256 devices in a mesh: gx: 32 (over x, z), gy: 8 (over y, core).
Axes of the slice: x: 4, y: 4, z: 8, core: 2. Of those that a mesh axis runs over, the one named last changes fastest.
Arguments:
- probes: bfloat16 [64, 256, 128, 128], P(None, 'gx', 'gy'), may hold values from -6 to 6
- permeability: float32 [256, 128, 128], P('gx', 'gy'), may hold values from 0.2 to 5
- absorption: float32 [256, 128, 128], P('gx', 'gy'), may hold values from 0.3 to 3
- sensitivity: float32 [256, 128, 128], P('gx', 'gy'), may hold values from -6 to 6
- observe_weight: float32 [256, 128, 128], P('gx', 'gy'), may hold values from 1 to 10
Outputs:
- q_basis: float32 [64, 256, 128, 128], P(None, 'gx', 'gy')
- r_factor: float32 [64, 64], replicated
The draws below stay inside these ranges and needn't reach their ends.
All inputs are finite; a program needn't handle non-finite values.
Results may differ from the reference program's by a relative error of at most 0.0003.
Values sent between devices are 32-bit elements; how exact they have to be, the bound alone decides.
A program may use at most 128 MiB of HBM per device.

```python
import math
import jax
import jax.numpy as jnp
from jax import lax

PROBES = 64
SWEEPS = 4
NX = 256
NY = 128
NZ = 128


def shard_levels(rng, dims, cuts, low, top_value):
    def one(position, blocks):
        steps = jax.random.uniform(jax.random.fold_in(jax.random.fold_in(rng, 6), position), (blocks,), jnp.float32, low / len(cuts), top_value / len(cuts))
        return jnp.repeat(jnp.exp(steps), dims[position] // blocks).reshape((-1,) + (1,) * (len(dims) - position - 1))

    level = one(*cuts[0])
    for cut in cuts[1:]:
        level = level * one(*cut)
    return level


def bell_draw(key, dims, spread, reach, pieces=(), held_as=jnp.bfloat16):
    drawn = spread * jax.random.normal(key, dims, jnp.float32)
    if pieces:
        drawn = drawn * shard_levels(key, dims, pieces, -0.22, 0.18)
    return jnp.clip(drawn, -reach, reach).astype(held_as)


def setup_inputs(seed: int = 0) -> dict:
    splits = jax.random.split(jax.random.key(seed), 6)
    probes = bell_draw(splits[0], (PROBES, NX, NY, NZ), 1.0, 6.0, ((1, 32), (2, 8)))
    permeability = jnp.clip(jnp.exp(math.log(5.0) - 3.218876 * jax.random.uniform(splits[1], (NX, NY, NZ), jnp.float32) ** shard_levels(splits[1], (NX, NY, NZ), ((0, 32), (1, 8)), -0.2, 0.2)), 0.2, 5.0)
    absorption = jnp.clip(jnp.exp(math.log(3.0) - 2.3025851 * jax.random.uniform(splits[2], (NX, NY, NZ), jnp.float32) ** shard_levels(splits[2], (NX, NY, NZ), ((0, 32), (1, 8)), -0.2, 0.2)), 0.3, 3.0)
    sensitivity = bell_draw(splits[3], (NX, NY, NZ), 1.0, 6.0, ((0, 32), (1, 8)), jnp.float32)
    observe_weight = jnp.clip(jnp.exp(math.log(10.0) - 2.3025851 * jax.random.uniform(splits[4], (NX, NY, NZ), jnp.float32) ** shard_levels(splits[4], (NX, NY, NZ), ((0, 32), (1, 8)), -0.2, 0.2)), 1.0, 10.0)
    return {"probes": probes, "permeability": permeability, "absorption": absorption, "sensitivity": sensitivity, "observe_weight": observe_weight}


def face_terms(kpad, absorption):
    center = kpad[1:-1, 1:-1]
    x_low = 0.5 * (center + kpad[:-2, 1:-1])
    x_high = 0.5 * (center + kpad[2:, 1:-1])
    y_low = 0.5 * (center + kpad[1:-1, :-2])
    y_high = 0.5 * (center + kpad[1:-1, 2:])
    zpad = jnp.pad(center, ((0, 0), (0, 0), (1, 1)))
    z_low = 0.5 * (center + zpad[:, :, :-2])
    z_high = 0.5 * (center + zpad[:, :, 2:])
    diag = absorption + x_low + x_high + y_low + y_high + z_low + z_high
    return ((x_low, x_high, y_low, y_high, z_low, z_high), diag)

def sweep(field, padded, rhs, coefs, diag):
    x_low, x_high, y_low, y_high, z_low, z_high = coefs
    zpad = jnp.pad(field, ((0, 0), (0, 0), (0, 0), (1, 1)))
    total = x_low * padded[:, :-2, 1:-1] + x_high * padded[:, 2:, 1:-1]
    total = total + y_low * padded[:, 1:-1, :-2] + y_high * padded[:, 1:-1, 2:]
    total = total + z_low * zpad[..., :-2] + z_high * zpad[..., 2:]
    return 0.2 * field + 0.8 * (rhs + total) / diag

def jacobi(rhs, coefs, diag):
    field = jnp.zeros_like(rhs)
    for step in range(SWEEPS):
        padded = jnp.pad(field, ((0, 0), (1, 1), (1, 1), (0, 0)))
        field = sweep(field, padded, rhs, coefs, diag)
    return field

def reference(probes, permeability, absorption, sensitivity, observe_weight):
    kpad = jnp.pad(permeability, ((1, 1), (1, 1), (0, 0)))
    coefs, diag = face_terms(kpad, absorption)

    def respond(block):
        forward = jacobi(sensitivity * block.astype(jnp.float32), coefs, diag)
        adjoint = jacobi(observe_weight * forward, coefs, diag)
        return sensitivity * adjoint
    groups = probes.reshape(PROBES // 8, 8, NX, NY, NZ)
    responses = lax.map(respond, groups).reshape(PROBES, NX * NY * NZ)
    gram = jnp.dot(responses.astype(jnp.float32), responses.T.astype(jnp.float32), precision=lax.Precision.HIGHEST, preferred_element_type=jnp.float32) / float(NX * NY * NZ)
    r_factor = jnp.linalg.cholesky(gram).T
    q_basis = lax.linalg.triangular_solve(r_factor, responses, left_side=True, lower=False, transpose_a=True)
    return (q_basis.reshape(PROBES, NX, NY, NZ), r_factor)
```

```python
import functools

import jax
import jax.numpy as jnp
from jax import lax
from jax.experimental import pallas as pl
from jax.experimental.pallas import tpu as pltpu
from jax.sharding import PartitionSpec as P

MESH = pl.DeviceIdType.MESH
GROUPS = 4
ROWS = 4
XLO, XHI, YLO, YHI = range(4)


def remote(src, dst, send, recv, where):
    return pltpu.make_async_remote_copy(
        src_ref=src, dst_ref=dst, send_sem=send, recv_sem=recv, device_id=where, device_id_type=MESH
    )


def respond_kernel(
    dims,
    probes, perm, absorption, sensitivity, weight,
    y_out, gram_out,
    field, rhs, stage, kpad, kface, khalo_x, khalo_y, natural, spread,
    slot_c, slot_y, slot_x, slot_z,
    k_send, k_recv, f_send, f_recv, r_send, r_recv,
):
    peers_x, peers_y, chips_x, chips_y, chips_z = dims
    count, wx, wy, wz = probes.shape
    size = count // GROUPS
    tiles = size // 8
    gx, gy = lax.axis_index("gx"), lax.axis_index("gy")
    cx, cz = gx // chips_z, gx % chips_z
    cy, core = gy // 2, gy % 2

    x_before = ((gx + peers_x - 1) % peers_x, gy)
    x_after = ((gx + 1) % peers_x, gy)
    y_before = (gx, (gy + peers_y - 1) % peers_y)
    y_after = (gx, (gy + 1) % peers_y)
    other_core = [(gx, cy * 2 + 1 - core)]
    other_y = [(gx, (cy + j) % chips_y * 2 + core) for j in range(1, chips_y)]
    other_x = [((cx + j) % chips_x * chips_z + cz, gy) for j in range(1, chips_x)]
    other_z = [(cx * chips_z + (cz + j) % chips_z, gy) for j in range(1, chips_z)]

    barrier = pltpu.get_barrier_semaphore()
    everyone = [x_before, x_after, y_before, y_after] + other_core + other_y + other_x + other_z
    for where in everyone:
        pl.semaphore_signal(barrier, inc=1, device_id=where, device_id_type=MESH)
    pl.semaphore_wait(barrier, len(everyone))

    kface[0] = perm[:, 0, :]
    kface[1] = perm[:, wy - 1, :]
    k_copies = [
        remote(perm.at[wx - 1], khalo_x.at[0], k_send.at[0], k_recv.at[0], x_after),
        remote(perm.at[0], khalo_x.at[1], k_send.at[1], k_recv.at[1], x_before),
        remote(kface.at[1], khalo_y.at[0], k_send.at[2], k_recv.at[2], y_after),
        remote(kface.at[0], khalo_y.at[1], k_send.at[3], k_recv.at[3], y_before),
    ]
    for copy in k_copies:
        copy.start()
    for copy in k_copies:
        copy.wait()

    has_x_low = jnp.where(gx > 0, 1.0, 0.0).astype(jnp.float32)
    has_x_high = jnp.where(gx < peers_x - 1, 1.0, 0.0).astype(jnp.float32)
    has_y_low = jnp.where(gy > 0, 1.0, 0.0).astype(jnp.float32)
    has_y_high = jnp.where(gy < peers_y - 1, 1.0, 0.0).astype(jnp.float32)

    center = perm[...]
    kpad[pl.ds(1, wx), pl.ds(8, wy), :] = center
    kpad[0, pl.ds(8, wy), :] = khalo_x[0] * has_x_low
    kpad[wx + 1, pl.ds(8, wy), :] = khalo_x[1] * has_x_high
    for x in range(wx):
        kpad[x + 1, 7:8, :] = khalo_y[0, x:x + 1, :] * has_y_low
        kpad[x + 1, wy + 8:wy + 9, :] = khalo_y[1, x:x + 1, :] * has_y_high
    lane = lax.broadcasted_iota(jnp.int32, (wx, wy, wz), 2)
    x_at = lax.broadcasted_iota(jnp.int32, (wx, wy, wz), 0)
    y_at = lax.broadcasted_iota(jnp.int32, (wx, wy, wz), 1)

    def turned(value, shift):
        flat = pltpu.roll(value.reshape(-1, wz), shift, 1)
        return flat.reshape(value.shape)

    x_low = 0.5 * (center + kpad[pl.ds(0, wx), pl.ds(8, wy), :])
    x_high = 0.5 * (center + kpad[pl.ds(2, wx), pl.ds(8, wy), :])
    y_low = 0.5 * (center + kpad[pl.ds(1, wx), pl.ds(7, wy), :])
    y_high = 0.5 * (center + kpad[pl.ds(1, wx), pl.ds(9, wy), :])
    z_low = 0.5 * (center + jnp.where(lane == 0, 0.0, turned(center, 1)))
    z_high = 0.5 * (center + jnp.where(lane == wz - 1, 0.0, turned(center, wz - 1)))
    diag = absorption[...] + x_low + x_high + y_low + y_high + z_low + z_high
    damp = 0.8 / diag
    natural[0] = damp * jnp.where(x_at == 0, x_low * has_x_low, x_low)
    natural[1] = damp * jnp.where(x_at == wx - 1, x_high * has_x_high, x_high)
    natural[2] = damp * jnp.where(y_at == 0, y_low * has_y_low, y_low)
    natural[3] = damp * jnp.where(y_at == wy - 1, y_high * has_y_high, y_high)
    natural[4] = damp * jnp.where(lane == 0, 0.0, z_low)
    natural[5] = damp * jnp.where(lane == wz - 1, 0.0, z_high)
    natural[6] = damp * weight[...]
    natural[7] = sensitivity[...]
    natural[8] = damp * sensitivity[...]

    def faces(k, g):
        half = k % 2
        slot = half * GROUPS + g
        mine = field.at[slot]
        sides = (
            (mine.at[wx, pl.ds(1, wy)], mine.at[0, pl.ds(1, wy)], x_after),
            (mine.at[1, pl.ds(1, wy)], mine.at[wx + 1, pl.ds(1, wy)], x_before),
            (mine.at[pl.ds(1, wx), wy], mine.at[pl.ds(1, wx), 0], y_after),
            (mine.at[pl.ds(1, wx), 1], mine.at[pl.ds(1, wx), wy + 1], y_before),
        )
        return [
            remote(src, dst, f_send.at[slot, i], f_recv.at[slot, i], where)
            for i, (src, dst, where) in enumerate(sides)
        ]

    def first(g, carry):
        def plane(x, carry):
            def one(p, carry):
                value = probes[g * size + p, x].astype(jnp.float32) * natural[8, x]
                stage[pl.ds(p, wy, stride=size), :] = value
                return carry

            lax.fori_loop(0, size, one, 0, unroll=True)
            value = stage[...].reshape(wy, size, wz)
            field[g, x + 1, pl.ds(1, wy)] = value
            rhs[g, x] = value
            return carry

        lax.fori_loop(0, wx, plane, 0)
        for copy in faces(0, g):
            copy.start()
        return carry

    lax.fori_loop(0, GROUPS, first, 0)

    def widen(x, carry):
        for j in range(8):
            block = natural[j, x]
            for y in range(wy):
                spread[j, x, y] = jnp.broadcast_to(block[y:y + 1, :], (8, wz))
        return carry

    lax.fori_loop(0, wx, widen, 0)

    def sweep(k, g, last):
        old, new = (k % 2) * GROUPS + g, ((k + 1) % 2) * GROUPS + g

        def some(i, carry):
            x, y = i // (wy // ROWS), (i % (wy // ROWS)) * ROWS
            shape = (ROWS, tiles, 8, wz)

            def near(dx, dy):
                return field[old, x + 1 + dx, pl.ds(y + 1 + dy, ROWS)].reshape(shape)

            def factor(j):
                return spread[j, x, pl.ds(y, ROWS)].reshape(ROWS, 1, 8, wz)

            here = near(0, 0)
            total = rhs[g, x, pl.ds(y, ROWS)].reshape(shape) + 0.2 * here
            total = total + factor(0) * near(-1, 0) + factor(1) * near(1, 0)
            total = total + factor(2) * near(0, -1) + factor(3) * near(0, 1)
            total = total + factor(4) * turned(here, 1) + factor(5) * turned(here, wz - 1)
            if last == 2:
                total = total * factor(7)
                high = total.reshape(ROWS, size, wz).astype(jnp.bfloat16)
                low = (total.reshape(ROWS, size, wz) - high.astype(jnp.float32)).astype(jnp.bfloat16)
                at = pl.multiple_of(g * size, size)
                y_out[x, pl.ds(y, ROWS), pl.ds(at, size), :] = high
                y_out[x, pl.ds(y, ROWS), pl.ds(count + at, size), :] = low
                return carry
            if last == 1:
                total = total * factor(6)
                rhs[g, x, pl.ds(y, ROWS)] = total.reshape(ROWS, size, wz)
            field[new, x + 1, pl.ds(y + 1, ROWS)] = total.reshape(ROWS, size, wz)
            return carry

        lax.fori_loop(0, wx * wy // ROWS, some, 0)

    def step(k, g, first_of_all, last):
        if not first_of_all:
            for copy in faces(k + 1, g):
                copy.wait_send()
        for copy in faces(k, g):
            copy.wait_recv()
        sweep(k, g, last)
        if last != 2:
            for copy in faces(k + 1, g):
                copy.start()

    def run(k, g, first_of_all, last):
        def body(g, carry):
            step(k, g, first_of_all, last)
            return carry
        lax.fori_loop(0, GROUPS, body, 0)

    run(0, None, True, 0)
    run(1, None, False, 0)
    run(2, None, False, 1)

    def middle(i, carry):
        step(3 + i // GROUPS, i % GROUPS, False, 0)
        return carry
    lax.fori_loop(0, 2 * GROUPS, middle, 0)
    run(5, None, False, 2)

    def drain(g, carry):
        for copy in faces(5, g):
            copy.wait_send()
        return carry
    lax.fori_loop(0, GROUPS, drain, 0)

    def add(i, acc):
        x, y = i // (wy // 2), (i % (wy // 2)) * 2
        both = jnp.concatenate([y_out[x, y], y_out[x, y + 1]], axis=1)
        return acc + lax.dot_general(
            both, both, (((1,), (1,)), ((), ())), preferred_element_type=jnp.float32
        )

    product = lax.fori_loop(0, wx * wy // 2, add, jnp.zeros((2 * count, 2 * count), jnp.float32))
    folded = product[:count] + product[count:]
    folded = folded + pltpu.roll(folded, count, 1)
    half = count // 2
    lane2 = lax.broadcasted_iota(jnp.int32, (half, 2 * count), 1)
    packed = jnp.where(lane2 < count, folded[:half], folded[half:])

    base = 0
    for slots, me, others in (
        (slot_c, core, other_core), (slot_y, cy, other_y), (slot_x, cx, other_x), (slot_z, cz, other_z)
    ):
        n = len(others) + 1
        slots[me] = packed
        copies = [
            remote(slots.at[me], slots.at[me], r_send.at[base + j], r_recv.at[base + j], where)
            for j, where in enumerate(others)
        ]
        for copy in copies:
            copy.start()
        for copy in copies:
            copy.wait()
        packed = slots[0]
        for j in range(1, n):
            packed = packed + slots[j]
        base += n - 1
    cells = float(wx * peers_x * wy * peers_y * wz)
    gram_out[...] = packed / cells


def basis_kernel(y_ref, gram_ref, q_ref, r_ref, mix, stage):
    count = q_ref.shape[0]
    half = count // 2
    wy, wz = q_ref.shape[2], q_ref.shape[3]

    @pl.when(pl.program_id(0) == 0)
    def _():
        packed = gram_ref[...]
        rows = lax.broadcasted_iota(jnp.int32, (count, 2 * count), 0)
        lanes = lax.broadcasted_iota(jnp.int32, (count, 2 * count), 1)
        whole = jnp.concatenate([packed, pltpu.roll(packed, count, 1)], axis=0)
        work = jnp.where(lanes < count, whole, jnp.where(lanes - count == rows, 1.0, 0.0))
        scale = jnp.zeros((count, 1), jnp.float32)
        tall = lax.broadcasted_iota(jnp.int32, (count, 1), 0)
        for k in range(count):
            row = work[k:k + 1, :]
            pivot = row[:, k:k + 1]
            column = jnp.where(tall > k, work[:, k:k + 1], 0.0)
            scale = jnp.where(tall == k, pivot, scale)
            work = work - column * (row / pivot)
        work = work * lax.rsqrt(scale)
        r_ref[...] = jnp.where(lanes >= rows, work, 0.0)[:, :count]
        inverse = jnp.where(lanes < count, pltpu.roll(work, count, 1), work)
        high = inverse.astype(jnp.bfloat16)
        low = (inverse - high.astype(jnp.float32)).astype(jnp.bfloat16)
        mix[:, :2 * count] = high
        mix[:, 2 * count:] = low

    weights = mix[...]
    for y in range(0, wy, 2):
        both = jnp.concatenate([y_ref[0, y], y_ref[0, y + 1]], axis=1)
        both = jnp.concatenate([both, both], axis=0)
        out = jnp.dot(weights, both, preferred_element_type=jnp.float32)
        stage[pl.ds(y, count, stride=wy), :] = out[:, :wz]
        stage[pl.ds(y + 1, count, stride=wy), :] = out[:, wz:]
    q_ref[:, 0] = stage[...].reshape(count, wy, wz)


def body(dims, probes, permeability, absorption, sensitivity, observe_weight):
    count, wx, wy, wz = probes.shape
    size = count // GROUPS
    peers_x, peers_y, chips_x, chips_y, chips_z = dims
    f32 = jnp.float32
    vmem = pl.BlockSpec(memory_space=pltpu.VMEM)
    hops = 1 + chips_y - 1 + chips_x - 1 + chips_z - 1
    half = count // 2
    responses, gram = pl.pallas_call(
        functools.partial(respond_kernel, dims),
        out_shape=(
            jax.ShapeDtypeStruct((wx, wy, 2 * count, wz), jnp.bfloat16),
            jax.ShapeDtypeStruct((half, 2 * count), f32),
        ),
        in_specs=[vmem] * 5,
        out_specs=(vmem, vmem),
        scratch_shapes=[
            pltpu.VMEM((2 * GROUPS, wx + 2, wy + 2, size, wz), f32),
            pltpu.VMEM((GROUPS, wx, wy, size, wz), f32),
            pltpu.VMEM((wy * size, wz), f32),
            pltpu.VMEM((wx + 2, wy + 16, wz), f32),
            pltpu.VMEM((2, wx, wz), f32),
            pltpu.VMEM((2, wy, wz), f32),
            pltpu.VMEM((2, wx, wz), f32),
            pltpu.VMEM((9, wx, wy, wz), f32),
            pltpu.VMEM((8, wx, wy, 8, wz), f32),
            pltpu.VMEM((2, half, 2 * count), f32),
            pltpu.VMEM((chips_y, half, 2 * count), f32),
            pltpu.VMEM((chips_x, half, 2 * count), f32),
            pltpu.VMEM((chips_z, half, 2 * count), f32),
            pltpu.SemaphoreType.DMA((4,)),
            pltpu.SemaphoreType.DMA((4,)),
            pltpu.SemaphoreType.DMA((2 * GROUPS, 4)),
            pltpu.SemaphoreType.DMA((2 * GROUPS, 4)),
            pltpu.SemaphoreType.DMA((hops,)),
            pltpu.SemaphoreType.DMA((hops,)),
        ],
        compiler_params=pltpu.CompilerParams(
            collective_id=0, has_side_effects=True, vmem_limit_bytes=52 * 2**20
        ),
    )(probes, permeability, absorption, sensitivity, observe_weight)

    q_basis, r_factor = pl.pallas_call(
        basis_kernel,
        grid=(wx,),
        out_shape=(
            jax.ShapeDtypeStruct((count, wx, wy, wz), f32),
            jax.ShapeDtypeStruct((count, count), f32),
        ),
        in_specs=[
            pl.BlockSpec((1, wy, 2 * count, wz), lambda i: (i, 0, 0, 0)),
            pl.BlockSpec((half, 2 * count), lambda i: (0, 0)),
        ],
        out_specs=(
            pl.BlockSpec((count, 1, wy, wz), lambda i: (0, i, 0, 0)),
            pl.BlockSpec((count, count), lambda i: (0, 0)),
        ),
        scratch_shapes=[
            pltpu.VMEM((count, 4 * count), jnp.bfloat16),
            pltpu.VMEM((count * wy, wz), f32),
        ],
        compiler_params=pltpu.CompilerParams(vmem_limit_bytes=32 * 2**20),
    )(responses, gram)
    return q_basis, r_factor


def solution(mesh):
    peers_x, peers_y = mesh.shape["gx"], mesh.shape["gy"]
    chips_x = 4
    dims = (peers_x, peers_y, chips_x, peers_y // 2, peers_x // chips_x)
    cell = P("gx", "gy", None)
    field = P(None, "gx", "gy", None)
    return jax.shard_map(
        functools.partial(body, dims),
        mesh=mesh,
        in_specs=(field, cell, cell, cell, cell),
        out_specs=(field, P()),
        check_vma=False,
    )
```

```python
import functools

import jax
import jax.numpy as jnp
from jax import lax
from jax.experimental import pallas as pl
from jax.experimental.pallas import tpu as pltpu
from jax.sharding import PartitionSpec as P

MESH = pl.DeviceIdType.MESH
GROUPS = 4
PANEL = 8


def remote(src, dst, send, recv, where):
    return pltpu.make_async_remote_copy(
        src_ref=src, dst_ref=dst, send_sem=send, recv_sem=recv, device_id=where, device_id_type=MESH
    )


def respond_kernel(
    dims,
    probes_hbm, perm_hbm, absorption_hbm, sensitivity_hbm, weight_hbm,
    y_hbm, gram_out,
    probes, perm, absorption, sensitivity, weight,
    raw, even, odd, rhs, y_out, stage, kpad, kface, khalo_x, khalo_y, sface, shalo_x, shalo_y,
    natural, spread, seed_row, product,
    slot_y, slot_x, slot_z,
    in_sem, out_sem, k_send, k_recv, s_send, s_recv, f_send, f_recv, r_send, r_recv,
):
    peers_x, peers_y, chips_x, chips_z = dims
    count, wx, wy, wz = probes.shape
    size = count // GROUPS
    tiles = size // 8
    gx, gy = lax.axis_index("gx"), lax.axis_index("gy")
    cx, cz = gx // chips_z, gx % chips_z

    x_before = ((gx + peers_x - 1) % peers_x, gy)
    x_after = ((gx + 1) % peers_x, gy)
    y_before = (gx, (gy + peers_y - 1) % peers_y)
    y_after = (gx, (gy + 1) % peers_y)
    other_y = [(gx, (gy + j) % peers_y) for j in range(1, peers_y)]
    other_x = [((cx + j) % chips_x * chips_z + cz, gy) for j in range(1, chips_x)]
    other_z = [(cx * chips_z + (cz + j) % chips_z, gy) for j in range(1, chips_z)]

    barrier = pltpu.get_barrier_semaphore()
    everyone = [x_before, x_after, y_before, y_after] + other_y + other_x + other_z
    for where in everyone:
        pl.semaphore_signal(barrier, inc=1, device_id=where, device_id_type=MESH)

    loads = [
        pltpu.make_async_copy(src, dst, in_sem.at[i])
        for i, (src, dst) in enumerate((
            (perm_hbm, perm), (absorption_hbm, absorption), (sensitivity_hbm, sensitivity), (weight_hbm, weight)
        ))
    ]

    def probe_load(g):
        at = pl.ds(g * size, size)
        return pltpu.make_async_copy(probes_hbm.at[at], probes.at[at], in_sem.at[4 + g])

    probe_load(0).start()
    loads[0].start()
    for g in range(1, GROUPS):
        probe_load(g).start()
    for load in loads[1:]:
        load.start()

    fields = (even, odd)

    def faces(e, g):
        mine = (fields[e % 2] if e else raw).at[g]
        sides = (
            (mine.at[wx, pl.ds(1, wy)], mine.at[0, pl.ds(1, wy)], x_after),
            (mine.at[1, pl.ds(1, wy)], mine.at[wx + 1, pl.ds(1, wy)], x_before),
            (mine.at[pl.ds(1, wx), wy], mine.at[pl.ds(1, wx), 0], y_after),
            (mine.at[pl.ds(1, wx), 1], mine.at[pl.ds(1, wx), wy + 1], y_before),
        )
        return [
            remote(src, dst, f_send.at[e % 2, g, i], f_recv.at[e % 2, g, i], where)
            for i, (src, dst, where) in enumerate(sides)
        ]

    def side_rows(pair, halo_x, halo_y, array, send, recv):
        return [
            remote(array.at[wx - 1], halo_x.at[0], send.at[0], recv.at[0], x_after),
            remote(array.at[0], halo_x.at[1], send.at[1], recv.at[1], x_before),
            remote(pair.at[1], halo_y.at[0], send.at[2], recv.at[2], y_after),
            remote(pair.at[0], halo_y.at[1], send.at[3], recv.at[3], y_before),
        ]

    def plane_of(g):
        def plane(x):
            def one(p, carry):
                stage[pl.ds(p, wy, stride=size), :] = probes[g * size + p, x].astype(jnp.float32)
                return carry

            lax.fori_loop(0, size, one, 0, unroll=True)
            raw[g, x + 1, pl.ds(1, wy)] = stage[...].reshape(wy, size, wz)

        return plane

    def outer_planes(g):
        plane = plane_of(g)

        def body(i, carry):
            plane(i * (wx - 1))
            return carry

        probe_load(g).wait()
        lax.fori_loop(0, 2, body, 0)

    def inner_planes(g):
        plane = plane_of(g)

        def body(x, carry):
            plane(x)
            return carry

        lax.fori_loop(1, wx - 1, body, 0)

    def send_x(g):
        for copy in faces(0, g)[:2]:
            copy.start()

    def send_y(g):
        for copy in faces(0, g)[2:]:
            copy.start()

    loads[0].wait()
    kface[0] = perm[:, 0, :]
    kface[1] = perm[:, wy - 1, :]
    k_copies = side_rows(kface, khalo_x, khalo_y, perm, k_send, k_recv)

    outer_planes(0)
    pl.semaphore_wait(barrier, len(everyone))
    for copy in k_copies:
        copy.start()
    send_x(0)
    outer_planes(1)
    send_x(1)
    inner_planes(0)
    send_y(0)
    inner_planes(1)
    send_y(1)

    for load in loads[1:]:
        load.wait()
    for copy in k_copies:
        copy.wait()

    has_x_low = jnp.where(gx > 0, 1.0, 0.0).astype(jnp.float32)
    has_x_high = jnp.where(gx < peers_x - 1, 1.0, 0.0).astype(jnp.float32)
    has_y_low = jnp.where(gy > 0, 1.0, 0.0).astype(jnp.float32)
    has_y_high = jnp.where(gy < peers_y - 1, 1.0, 0.0).astype(jnp.float32)

    center = perm[...]
    kpad[pl.ds(1, wx), pl.ds(8, wy), :] = center
    kpad[0, pl.ds(8, wy), :] = khalo_x[0] * has_x_low
    kpad[wx + 1, pl.ds(8, wy), :] = khalo_x[1] * has_x_high
    for x in range(wx):
        kpad[x + 1, 7:8, :] = khalo_y[0, x:x + 1, :] * has_y_low
        kpad[x + 1, wy + 8:wy + 9, :] = khalo_y[1, x:x + 1, :] * has_y_high
    lane = lax.broadcasted_iota(jnp.int32, (wx, wy, wz), 2)
    x_at = lax.broadcasted_iota(jnp.int32, (wx, wy, wz), 0)
    y_at = lax.broadcasted_iota(jnp.int32, (wx, wy, wz), 1)

    def turned(value, shift):
        flat = pltpu.roll(value.reshape(-1, wz), shift, 1)
        return flat.reshape(value.shape)

    x_low = 0.5 * (center + kpad[pl.ds(0, wx), pl.ds(8, wy), :])
    x_high = 0.5 * (center + kpad[pl.ds(2, wx), pl.ds(8, wy), :])
    y_low = 0.5 * (center + kpad[pl.ds(1, wx), pl.ds(7, wy), :])
    y_high = 0.5 * (center + kpad[pl.ds(1, wx), pl.ds(9, wy), :])
    z_low = 0.5 * (center + jnp.where(lane == 0, 0.0, turned(center, 1)))
    z_high = 0.5 * (center + jnp.where(lane == wz - 1, 0.0, turned(center, wz - 1)))
    diag = absorption[...] + x_low + x_high + y_low + y_high + z_low + z_high
    damp = 0.8 / diag
    seed = damp * sensitivity[...]
    natural[8] = seed
    sface[0] = seed[:, 0, :]
    sface[1] = seed[:, wy - 1, :]
    s_copies = side_rows(sface, shalo_x, shalo_y, natural.at[8], s_send, s_recv)
    for copy in s_copies:
        copy.start()
    for g in range(2, GROUPS):
        outer_planes(g)
        send_x(g)
    for g in range(2, GROUPS):
        inner_planes(g)
        send_y(g)
    natural[0] = damp * jnp.where(x_at == 0, x_low * has_x_low, x_low)
    natural[1] = damp * jnp.where(x_at == wx - 1, x_high * has_x_high, x_high)
    natural[2] = damp * jnp.where(y_at == 0, y_low * has_y_low, y_low)
    natural[3] = damp * jnp.where(y_at == wy - 1, y_high * has_y_high, y_high)
    natural[4] = damp * jnp.where(lane == 0, 0.0, z_low)
    natural[5] = damp * jnp.where(lane == wz - 1, 0.0, z_high)
    natural[6] = damp * weight[...]
    natural[7] = sensitivity[...]

    def widen(x, carry):
        for j in range(9):
            block = natural[j, x]
            for y in range(wy):
                row = jnp.broadcast_to(block[y:y + 1, :], (8, wz))
                if j < 8:
                    spread[j, x, y] = row
                else:
                    seed_row[x + 1, y + 1] = row
        return carry

    lax.fori_loop(0, wx, widen, 0)
    for copy in s_copies:
        copy.wait()
    for side in range(2):
        for y in range(wy):
            seed_row[side * (wx + 1), y + 1] = jnp.broadcast_to(shalo_x[side, y:y + 1, :], (8, wz))
        for x in range(wx):
            seed_row[x + 1, side * (wy + 1)] = jnp.broadcast_to(shalo_y[side, x:x + 1, :], (8, wz))

    def seeded(g, at_x, at_y, n):
        value = raw[g, at_x, at_y].reshape(n, tiles, 8, wz) * seed_row[at_x, at_y].reshape(n, 1, 8, wz)
        return value.reshape(n, size, wz)

    def inside(g, carry):
        def plane(x, carry):
            value = seeded(g, x + 1, pl.ds(1, wy), wy)
            even[g, x + 1, pl.ds(1, wy)] = value
            rhs[g, x] = value
            return carry

        lax.fori_loop(0, wx, plane, 0)
        return carry

    lax.fori_loop(0, GROUPS, inside, 0)

    def sweep(e, g, last):
        old, new = fields[e % 2], fields[(e + 1) % 2]
        shape = (wy, tiles, 8, wz)

        def plane(x, carry):
            def near(dx, dy):
                return old[g, x + 1 + dx, pl.ds(1 + dy, wy)].reshape(shape)

            def factor(j):
                return spread[j, x].reshape(wy, 1, 8, wz)

            here = near(0, 0)
            total = rhs[g, x].reshape(shape) + 0.2 * here
            total = total + factor(0) * near(-1, 0) + factor(1) * near(1, 0)
            total = total + factor(2) * near(0, -1) + factor(3) * near(0, 1)
            total = total + factor(4) * turned(here, 1) + factor(5) * turned(here, wz - 1)
            if last == 2:
                total = (total * factor(7)).reshape(wy, size, wz)
                high = total.astype(jnp.bfloat16)
                low = (total - high.astype(jnp.float32)).astype(jnp.bfloat16)
                y_out[x, :, pl.ds(2 * g * size, size), :] = high
                y_out[x, :, pl.ds((2 * g + 1) * size, size), :] = low
                return carry
            if last == 1:
                total = total * factor(6)
                rhs[g, x] = total.reshape(wy, size, wz)
            new[g, x + 1, pl.ds(1, wy)] = total.reshape(wy, size, wz)
            return carry

        lax.fori_loop(0, wx, plane, 0)

    def step(e, g):
        if e:
            for copy in faces(e - 1, g):
                copy.wait_send()
        for copy in faces(e, g):
            copy.wait_recv()
        if e == 0:
            for side in range(2):
                x, y = side * (wx + 1), side * (wy + 1)
                even[g, x, pl.ds(1, wy)] = seeded(g, x, pl.ds(1, wy), wy)
                even[g, pl.ds(1, wx), y] = seeded(g, pl.ds(1, wx), y, wx)
        sweep(e, g, 1 if e == 2 else 2 if e == 5 else 0)
        if e < 5:
            for copy in faces(e + 1, g):
                copy.start()

    def run(e):
        def body(g, carry):
            step(e, g)
            return carry
        lax.fori_loop(0, GROUPS, body, 0)

    for e in range(5):
        run(e)

    def y_write(g):
        at = pl.ds(2 * size * g, 2 * size)
        return pltpu.make_async_copy(y_out.at[:, :, at], y_hbm.at[:, :, at], out_sem.at[g])

    for g in range(GROUPS):
        step(5, g)
        for copy in faces(5, g):
            copy.wait_send()
        y_write(g).start()
        high_row = 2 * size * (g + 1)

        def add(x, acc):
            for y in range(0, wy, 2):
                both = jnp.concatenate([y_out[x, y, :high_row], y_out[x, y + 1, :high_row]], axis=1)
                acc = acc + lax.dot_general(
                    both, both[2 * size * g:], (((1,), (1,)), ((), ())), preferred_element_type=jnp.float32
                )
            return acc

        block = lax.fori_loop(0, wx, add, jnp.zeros((high_row, 2 * size), jnp.float32))
        product[:high_row, 2 * size * g:high_row] = block
        if g + 1 < GROUPS:
            product[high_row:, 2 * size * g:high_row] = jnp.zeros((2 * count - high_row, 2 * size), jnp.float32)

    folded = product[...].reshape(GROUPS, 2, size, 2 * count)
    folded = (folded[:, 0] + folded[:, 1]).reshape(count, 2 * count)
    twice = jnp.dot(
        folded, parts_of(2 * count, 2 * count, size, True),
        precision=lax.Precision.HIGHEST, preferred_element_type=jnp.float32,
    )
    half = count // 2
    first_half = lax.broadcasted_iota(jnp.int32, (half, 2 * count), 1) < count
    packed = jnp.where(first_half, twice[:half], twice[half:])
    base, sent = 0, []
    for slots, me, others in (
        (slot_y, gy, other_y), (slot_x, cx, other_x), (slot_z, cz, other_z)
    ):
        n = len(others) + 1
        slots[me] = packed
        copies = [
            remote(slots.at[me], slots.at[me], r_send.at[base + j], r_recv.at[base + j], where)
            for j, where in enumerate(others)
        ]
        for copy in copies:
            copy.start()
        sent += copies
        for copy in copies:
            copy.wait_recv()
        packed = slots[0]
        for j in range(1, n):
            packed = packed + slots[j]
        base += n - 1
    cells = float(wx * peers_x * wy * peers_y * wz)
    gram_out[...] = packed / cells
    for copy in sent:
        copy.wait_send()
    for g in range(GROUPS):
        y_write(g).wait()


def parts_of(height, width, size, from_parts):
    row, lane = (lax.broadcasted_iota(jnp.int32, (height, width), d) for d in (0, 1))
    part, number = (row, lane) if from_parts else (lane, row)
    count = width // 2
    of_part = part // (2 * size) * size + part % size
    return jnp.where(of_part == number % count, 1.0, 0.0).astype(jnp.float32)


def basis_kernel(y_hbm, gram_ref, q_ref, r_ref, y_ref, mix, stage, y_sem):
    count = q_ref.shape[0]
    half = count // 2
    size = count // GROUPS
    wy, wz = q_ref.shape[2], q_ref.shape[3]
    x = pl.program_id(0)

    @pl.when(x == 0)
    def _():
        y_read = pltpu.make_async_copy(y_hbm, y_ref, y_sem)
        y_read.start()
        packed = gram_ref[...]
        wide = (count, 2 * count)
        rows, lanes = (lax.broadcasted_iota(jnp.int32, wide, d) for d in (0, 1))
        upper = jnp.concatenate([packed, pltpu.roll(packed, count, 1)], axis=0)
        turned = jnp.transpose(jnp.concatenate([upper, upper], axis=0))[:count]
        whole = jnp.where(lanes // size >= rows // size, upper, turned)
        work = jnp.where(lanes < count, whole, jnp.where(lanes - count == rows, 1.0, 0.0))
        pivots, done = [], []
        for base in range(0, count, PANEL):
            height = count - base
            below = lax.broadcasted_iota(jnp.int32, (height, 2 * count), 0)
            columns = [
                jnp.broadcast_to(work[:, base + k:base + k + 1], (height, 2 * count)) for k in range(PANEL)
            ]
            for k in range(PANEL):
                pivot = columns[k][k:k + 1]
                pivots.append(pivot)
                inverse = 1.0 / pivot
                column = jnp.where(below > k, columns[k], 0.0)
                for m in range(k + 1, PANEL):
                    columns[m] = columns[m] - column * (columns[m][k:k + 1] * inverse)
                work = work - column * (work[k:k + 1] * inverse)
            done.append(work[:PANEL])
            work = work[PANEL:]
        work = jnp.concatenate(done, axis=0) * lax.rsqrt(jnp.concatenate(pivots, axis=0))
        r_ref[...] = jnp.where(lanes >= rows, work, 0.0)[:, :count]
        inverse = pltpu.roll(work, count, 1)[:, :count]
        high = inverse.astype(jnp.bfloat16)
        low = (inverse - high.astype(jnp.float32)).astype(jnp.bfloat16)
        place = parts_of(count, 2 * count, size, False).astype(jnp.bfloat16)
        mix[:, :2 * count] = jnp.dot(high, place, preferred_element_type=jnp.float32).astype(jnp.bfloat16)
        mix[:, 2 * count:] = jnp.dot(low, place, preferred_element_type=jnp.float32).astype(jnp.bfloat16)
        y_read.wait()

    weights = mix[...]
    for y in range(0, wy, 2):
        both = jnp.concatenate([y_ref[x, y], y_ref[x, y + 1]], axis=1)
        both = jnp.concatenate([both, both], axis=0)
        out = jnp.dot(weights, both, preferred_element_type=jnp.float32)
        stage[pl.ds(y, count, stride=wy), :] = out[:, :wz]
        stage[pl.ds(y + 1, count, stride=wy), :] = out[:, wz:]
    q_ref[:, 0] = stage[...].reshape(count, wy, wz)


def body(dims, probes, permeability, absorption, sensitivity, observe_weight):
    count, wx, wy, wz = probes.shape
    size = count // GROUPS
    peers_x, peers_y, chips_x, chips_z = dims
    f32 = jnp.float32
    vmem = pl.BlockSpec(memory_space=pltpu.VMEM)
    hops = peers_y - 1 + chips_x - 1 + chips_z - 1
    half = count // 2
    padded = pltpu.VMEM((GROUPS, wx + 2, wy + 2, size, wz), f32)
    responses, gram = pl.pallas_call(
        functools.partial(respond_kernel, dims),
        out_shape=(
            jax.ShapeDtypeStruct((wx, wy, 2 * count, wz), jnp.bfloat16),
            jax.ShapeDtypeStruct((half, 2 * count), f32),
        ),
        in_specs=[pl.BlockSpec(memory_space=pl.ANY)] * 5,
        out_specs=(pl.BlockSpec(memory_space=pl.ANY), vmem),
        scratch_shapes=[
            pltpu.VMEM((count, wx, wy, wz), jnp.bfloat16),
            pltpu.VMEM((wx, wy, wz), f32),
            pltpu.VMEM((wx, wy, wz), f32),
            pltpu.VMEM((wx, wy, wz), f32),
            pltpu.VMEM((wx, wy, wz), f32),
            padded,
            padded,
            padded,
            pltpu.VMEM((GROUPS, wx, wy, size, wz), f32),
            pltpu.VMEM((wx, wy, 2 * count, wz), jnp.bfloat16),
            pltpu.VMEM((wy * size, wz), f32),
            pltpu.VMEM((wx + 2, wy + 16, wz), f32),
            pltpu.VMEM((2, wx, wz), f32),
            pltpu.VMEM((2, wy, wz), f32),
            pltpu.VMEM((2, wx, wz), f32),
            pltpu.VMEM((2, wx, wz), f32),
            pltpu.VMEM((2, wy, wz), f32),
            pltpu.VMEM((2, wx, wz), f32),
            pltpu.VMEM((9, wx, wy, wz), f32),
            pltpu.VMEM((8, wx, wy, 8, wz), f32),
            pltpu.VMEM((wx + 2, wy + 2, 8, wz), f32),
            pltpu.VMEM((2 * count, 2 * count), f32),
            pltpu.VMEM((peers_y, half, 2 * count), f32),
            pltpu.VMEM((chips_x, half, 2 * count), f32),
            pltpu.VMEM((chips_z, half, 2 * count), f32),
            pltpu.SemaphoreType.DMA((4 + GROUPS,)),
            pltpu.SemaphoreType.DMA((GROUPS,)),
            pltpu.SemaphoreType.DMA((4,)),
            pltpu.SemaphoreType.DMA((4,)),
            pltpu.SemaphoreType.DMA((4,)),
            pltpu.SemaphoreType.DMA((4,)),
            pltpu.SemaphoreType.DMA((2, GROUPS, 4)),
            pltpu.SemaphoreType.DMA((2, GROUPS, 4)),
            pltpu.SemaphoreType.DMA((hops,)),
            pltpu.SemaphoreType.DMA((hops,)),
        ],
        compiler_params=pltpu.CompilerParams(
            collective_id=0, has_side_effects=True, vmem_limit_bytes=60 * 2**20
        ),
    )(probes, permeability, absorption, sensitivity, observe_weight)

    q_basis, r_factor = pl.pallas_call(
        basis_kernel,
        grid=(wx,),
        out_shape=(
            jax.ShapeDtypeStruct((count, wx, wy, wz), f32),
            jax.ShapeDtypeStruct((count, count), f32),
        ),
        in_specs=[
            pl.BlockSpec(memory_space=pl.ANY),
            pl.BlockSpec((half, 2 * count), lambda i: (0, 0)),
        ],
        out_specs=(
            pl.BlockSpec((count, 1, wy, wz), lambda i: (0, i, 0, 0)),
            pl.BlockSpec((count, count), lambda i: (0, 0)),
        ),
        scratch_shapes=[
            pltpu.VMEM((wx, wy, 2 * count, wz), jnp.bfloat16),
            pltpu.VMEM((count, 4 * count), jnp.bfloat16),
            pltpu.VMEM((count * wy, wz), f32),
            pltpu.SemaphoreType.DMA,
        ],
        compiler_params=pltpu.CompilerParams(vmem_limit_bytes=60 * 2**20),
    )(responses, gram)
    return q_basis, r_factor


def solution(mesh):
    peers_x, peers_y = mesh.shape["gx"], mesh.shape["gy"]
    chips_x = 4
    dims = (peers_x, peers_y, chips_x, peers_x // chips_x)
    cell = P("gx", "gy", None)
    field = P(None, "gx", "gy", None)
    return jax.shard_map(
        functools.partial(body, dims),
        mesh=mesh,
        in_specs=(field, cell, cell, cell, cell),
        out_specs=(field, P()),
        check_vma=False,
    )
```

```python
import functools

import jax
import jax.numpy as jnp
from jax import lax
from jax.experimental import pallas as pl
from jax.experimental.pallas import tpu as pltpu
from jax.sharding import PartitionSpec as P

MESH = pl.DeviceIdType.MESH
GROUPS = 4
PANEL = 8


def remote(src, dst, send, recv, where):
    return pltpu.make_async_remote_copy(
        src_ref=src, dst_ref=dst, send_sem=send, recv_sem=recv, device_id=where, device_id_type=MESH
    )


def respond_kernel(
    dims,
    probes_hbm, perm_hbm, absorption_hbm, sensitivity_hbm, weight_hbm,
    y_hbm, gram_out,
    probes, perm, absorption, sensitivity, weight,
    raw, even, odd, rhs, y_out, stage, kpad, kface, khalo_x, khalo_y, sface, shalo_x, shalo_y,
    natural, spread, seed_row, product,
    slot_y, slot_x, slot_z,
    in_sem, out_sem, k_send, k_recv, s_send, s_recv, f_send, f_recv, r_send, r_recv,
):
    peers_x, peers_y, chips_x, chips_z = dims
    count, wx, wy, wz = probes.shape
    size = count // GROUPS
    tiles = size // 8
    gx, gy = lax.axis_index("gx"), lax.axis_index("gy")
    cx, cz = gx // chips_z, gx % chips_z

    x_before = ((gx + peers_x - 1) % peers_x, gy)
    x_after = ((gx + 1) % peers_x, gy)
    y_before = (gx, (gy + peers_y - 1) % peers_y)
    y_after = (gx, (gy + 1) % peers_y)
    def far_first(n):
        return sorted(range(1, n), key=lambda j: -min(j, n - j))

    other_y = [(gx, (gy + j) % peers_y) for j in far_first(peers_y)]
    other_x = [((cx + j) % chips_x * chips_z + cz, gy) for j in far_first(chips_x)]
    other_z = [(cx * chips_z + (cz + j) % chips_z, gy) for j in far_first(chips_z)]

    barrier = pltpu.get_barrier_semaphore()
    everyone = [x_before, x_after, y_before, y_after] + other_y + other_x + other_z
    for where in everyone:
        pl.semaphore_signal(barrier, inc=1, device_id=where, device_id_type=MESH)

    loads = [
        pltpu.make_async_copy(src, dst, in_sem.at[i])
        for i, (src, dst) in enumerate((
            (perm_hbm, perm), (absorption_hbm, absorption), (sensitivity_hbm, sensitivity), (weight_hbm, weight)
        ))
    ]

    def probe_load(g):
        at = pl.ds(g * size, size)
        return pltpu.make_async_copy(probes_hbm.at[at], probes.at[at], in_sem.at[4 + g])

    probe_load(0).start()
    loads[0].start()
    for g in range(1, GROUPS):
        probe_load(g).start()
    for load in loads[1:]:
        load.start()

    fields = (even, odd)

    def faces(e, g):
        mine = (fields[e % 2] if e else raw).at[g]
        sides = (
            (mine.at[wx, pl.ds(1, wy)], mine.at[0, pl.ds(1, wy)], x_after),
            (mine.at[1, pl.ds(1, wy)], mine.at[wx + 1, pl.ds(1, wy)], x_before),
            (mine.at[pl.ds(1, wx), wy], mine.at[pl.ds(1, wx), 0], y_after),
            (mine.at[pl.ds(1, wx), 1], mine.at[pl.ds(1, wx), wy + 1], y_before),
        )
        return [
            remote(src, dst, f_send.at[e % 2, g, i], f_recv.at[e % 2, g, i], where)
            for i, (src, dst, where) in enumerate(sides)
        ]

    def side_rows(pair, halo_x, halo_y, array, send, recv):
        return [
            remote(array.at[wx - 1], halo_x.at[0], send.at[0], recv.at[0], x_after),
            remote(array.at[0], halo_x.at[1], send.at[1], recv.at[1], x_before),
            remote(pair.at[1], halo_y.at[0], send.at[2], recv.at[2], y_after),
            remote(pair.at[0], halo_y.at[1], send.at[3], recv.at[3], y_before),
        ]

    def plane_of(g):
        def plane(x):
            def one(p, carry):
                stage[pl.ds(p, wy, stride=size), :] = probes[g * size + p, x].astype(jnp.float32)
                return carry

            lax.fori_loop(0, size, one, 0, unroll=True)
            raw[g, x + 1, pl.ds(1, wy)] = stage[...].reshape(wy, size, wz)

        return plane

    def outer_planes(g):
        plane = plane_of(g)

        def body(i, carry):
            plane(i * (wx - 1))
            return carry

        probe_load(g).wait()
        lax.fori_loop(0, 2, body, 0)

    def inner_planes(g):
        plane = plane_of(g)

        def body(x, carry):
            plane(x)
            return carry

        lax.fori_loop(1, wx - 1, body, 0)

    def send_x(g):
        for copy in faces(0, g)[:2]:
            copy.start()

    def send_y(g):
        for copy in faces(0, g)[2:]:
            copy.start()

    loads[0].wait()
    kface[0] = perm[:, 0, :]
    kface[1] = perm[:, wy - 1, :]
    k_copies = side_rows(kface, khalo_x, khalo_y, perm, k_send, k_recv)

    outer_planes(0)
    pl.semaphore_wait(barrier, len(everyone))
    for copy in k_copies:
        copy.start()
    send_x(0)
    outer_planes(1)
    send_x(1)
    inner_planes(0)
    send_y(0)
    inner_planes(1)
    send_y(1)

    for load in loads[1:]:
        load.wait()
    for copy in k_copies:
        copy.wait()

    has_x_low = jnp.where(gx > 0, 1.0, 0.0).astype(jnp.float32)
    has_x_high = jnp.where(gx < peers_x - 1, 1.0, 0.0).astype(jnp.float32)
    has_y_low = jnp.where(gy > 0, 1.0, 0.0).astype(jnp.float32)
    has_y_high = jnp.where(gy < peers_y - 1, 1.0, 0.0).astype(jnp.float32)

    center = perm[...]
    kpad[pl.ds(1, wx), pl.ds(8, wy), :] = center
    kpad[0, pl.ds(8, wy), :] = khalo_x[0] * has_x_low
    kpad[wx + 1, pl.ds(8, wy), :] = khalo_x[1] * has_x_high
    for x in range(wx):
        kpad[x + 1, 7:8, :] = khalo_y[0, x:x + 1, :] * has_y_low
        kpad[x + 1, wy + 8:wy + 9, :] = khalo_y[1, x:x + 1, :] * has_y_high
    lane = lax.broadcasted_iota(jnp.int32, (wx, wy, wz), 2)
    x_at = lax.broadcasted_iota(jnp.int32, (wx, wy, wz), 0)
    y_at = lax.broadcasted_iota(jnp.int32, (wx, wy, wz), 1)

    def turned(value, shift):
        flat = pltpu.roll(value.reshape(-1, wz), shift, 1)
        return flat.reshape(value.shape)

    x_low = 0.5 * (center + kpad[pl.ds(0, wx), pl.ds(8, wy), :])
    x_high = 0.5 * (center + kpad[pl.ds(2, wx), pl.ds(8, wy), :])
    y_low = 0.5 * (center + kpad[pl.ds(1, wx), pl.ds(7, wy), :])
    y_high = 0.5 * (center + kpad[pl.ds(1, wx), pl.ds(9, wy), :])
    z_low = 0.5 * (center + jnp.where(lane == 0, 0.0, turned(center, 1)))
    z_high = 0.5 * (center + jnp.where(lane == wz - 1, 0.0, turned(center, wz - 1)))
    diag = absorption[...] + x_low + x_high + y_low + y_high + z_low + z_high
    damp = 0.8 / diag
    seed = damp * sensitivity[...]
    natural[8] = seed
    sface[0] = seed[:, 0, :]
    sface[1] = seed[:, wy - 1, :]
    s_copies = side_rows(sface, shalo_x, shalo_y, natural.at[8], s_send, s_recv)
    for copy in s_copies:
        copy.start()
    for g in range(2, GROUPS):
        outer_planes(g)
        send_x(g)
    for g in range(2, GROUPS):
        inner_planes(g)
        send_y(g)
    natural[0] = damp * jnp.where(x_at == 0, x_low * has_x_low, x_low)
    natural[1] = damp * jnp.where(x_at == wx - 1, x_high * has_x_high, x_high)
    natural[2] = damp * jnp.where(y_at == 0, y_low * has_y_low, y_low)
    natural[3] = damp * jnp.where(y_at == wy - 1, y_high * has_y_high, y_high)
    natural[4] = damp * jnp.where(lane == 0, 0.0, z_low)
    natural[5] = damp * jnp.where(lane == wz - 1, 0.0, z_high)
    natural[6] = damp * weight[...]
    natural[7] = sensitivity[...]

    def widen(x, carry):
        for j in range(9):
            block = natural[j, x]
            for y in range(wy):
                row = jnp.broadcast_to(block[y:y + 1, :], (8, wz))
                if j < 8:
                    spread[j, x, y] = row
                else:
                    seed_row[x + 1, y + 1] = row
        return carry

    lax.fori_loop(0, wx, widen, 0)
    for copy in s_copies:
        copy.wait()
    for side in range(2):
        for y in range(wy):
            seed_row[side * (wx + 1), y + 1] = jnp.broadcast_to(shalo_x[side, y:y + 1, :], (8, wz))
        for x in range(wx):
            seed_row[x + 1, side * (wy + 1)] = jnp.broadcast_to(shalo_y[side, x:x + 1, :], (8, wz))

    def seeded(g, at_x, at_y, n):
        value = raw[g, at_x, at_y].reshape(n, tiles, 8, wz) * seed_row[at_x, at_y].reshape(n, 1, 8, wz)
        return value.reshape(n, size, wz)

    def inside(g, carry):
        def plane(x, carry):
            value = seeded(g, x + 1, pl.ds(1, wy), wy)
            even[g, x + 1, pl.ds(1, wy)] = value
            rhs[g, x] = value
            return carry

        lax.fori_loop(0, wx, plane, 0)
        return carry

    lax.fori_loop(0, GROUPS, inside, 0)

    def sweep(e, g, last):
        old, new = fields[e % 2], fields[(e + 1) % 2]
        shape = (wy, tiles, 8, wz)

        def plane(x):
            def near(dx, dy):
                return old[g, x + 1 + dx, pl.ds(1 + dy, wy)].reshape(shape)

            def factor(j):
                return spread[j, x].reshape(wy, 1, 8, wz)

            here = near(0, 0)
            total = rhs[g, x].reshape(shape) + 0.2 * here
            total = total + factor(0) * near(-1, 0) + factor(1) * near(1, 0)
            total = total + factor(2) * near(0, -1) + factor(3) * near(0, 1)
            total = total + factor(4) * turned(here, 1) + factor(5) * turned(here, wz - 1)
            if last == 2:
                total = (total * factor(7)).reshape(wy, size, wz)
                high = total.astype(jnp.bfloat16).astype(jnp.float32)
                parts = jnp.concatenate([high, total - high], axis=1).astype(jnp.bfloat16)
                y_out[x, :, pl.ds(2 * g * size, 2 * size), :] = parts
                return
            if last == 1:
                total = total * factor(6)
                rhs[g, x] = total.reshape(wy, size, wz)
            new[g, x + 1, pl.ds(1, wy)] = total.reshape(wy, size, wz)

        def planes(x, carry):
            plane(x)
            return carry

        lax.fori_loop(0, wx, planes, 0)

    def step(e, g):
        if e:
            for copy in faces(e - 1, g):
                copy.wait_send()
        for copy in faces(e, g):
            copy.wait_recv()
        if e == 0:
            for side in range(2):
                x, y = side * (wx + 1), side * (wy + 1)
                even[g, x, pl.ds(1, wy)] = seeded(g, x, pl.ds(1, wy), wy)
                even[g, pl.ds(1, wx), y] = seeded(g, pl.ds(1, wx), y, wx)
        sweep(e, g, 1 if e == 2 else 2 if e == 5 else 0)
        if e < 5:
            for copy in faces(e + 1, g):
                copy.start()

    def run(e):
        def body(g, carry):
            step(e, g)
            return carry
        lax.fori_loop(0, GROUPS, body, 0)

    for e in range(5):
        run(e)

    def y_write(g):
        at = pl.ds(2 * size * g, 2 * size)
        return pltpu.make_async_copy(y_out.at[:, :, at], y_hbm.at[:, :, at], out_sem.at[g])

    for g in range(GROUPS):
        step(5, g)
        for copy in faces(5, g):
            copy.wait_send()
        y_write(g).start()
        high_row = 2 * size * (g + 1)

        def add(x, acc):
            for y in range(0, wy, 2):
                both = jnp.concatenate([y_out[x, y, :high_row], y_out[x, y + 1, :high_row]], axis=1)
                acc = acc + lax.dot_general(
                    both[2 * size * g:], both, (((1,), (1,)), ((), ())), preferred_element_type=jnp.float32
                )
            return acc

        block = lax.fori_loop(0, wx, add, jnp.zeros((2 * size, high_row), jnp.float32))
        product[2 * size * g:high_row, :high_row] = block
        if g + 1 < GROUPS:
            product[2 * size * g:high_row, high_row:] = jnp.zeros((2 * size, 2 * count - high_row), jnp.float32)

    folded = product[...].reshape(GROUPS, 2, size, 2 * count)
    folded = (folded[:, 0] + folded[:, 1]).reshape(count, 2 * count)
    folded = folded + pltpu.roll(folded, 2 * count - size, 1)
    half = count // 2
    first_half = lax.broadcasted_iota(jnp.int32, (half, 2 * count), 1) % (2 * size) < size
    packed = jnp.where(first_half, folded[:half], pltpu.roll(folded[half:], size, 1))
    base, sent = 0, []
    for slots, me, others in (
        (slot_y, gy, other_y), (slot_x, cx, other_x), (slot_z, cz, other_z)
    ):
        n = len(others) + 1
        slots[me] = packed
        copies = [
            remote(slots.at[me], slots.at[me], r_send.at[base + j], r_recv.at[base + j], where)
            for j, where in enumerate(others)
        ]
        for copy in copies:
            copy.start()
        sent += copies
        for copy in copies:
            copy.wait_recv()
        packed = slots[0]
        for j in range(1, n):
            packed = packed + slots[j]
        base += n - 1
    cells = float(wx * peers_x * wy * peers_y * wz)
    gram_out[...] = packed / cells
    for copy in sent:
        copy.wait_send()
    for g in range(GROUPS):
        y_write(g).wait()


def basis_kernel(y_hbm, gram_ref, q_ref, r_ref, y_ref, mix, stage, y_sem, q_sem):
    count = q_ref.shape[0]
    wx = q_ref.shape[1]
    half = count // 2
    size = count // GROUPS
    wy, wz = q_ref.shape[2], q_ref.shape[3]

    def y_read(n):
        return pltpu.make_async_copy(y_hbm.at[n], y_ref.at[n], y_sem.at[n])

    for n in range(wx):
        y_read(n).start()
    packed = gram_ref[...]
    wide = (count, 2 * count)
    rows, lanes = (lax.broadcasted_iota(jnp.int32, wide, d) for d in (0, 1))
    lower = jnp.concatenate([packed, pltpu.roll(packed, 2 * count - size, 1)], axis=0)
    pairs = lower.reshape(GROUPS, 1, size, 2 * count)
    turned = jnp.transpose(jnp.concatenate([pairs, pairs], axis=1).reshape(2 * count, 2 * count))
    turned = turned.reshape(GROUPS, 2, size, 2 * count)[:, 0].reshape(count, 2 * count)
    in_gram = lanes % (2 * size) < size
    number = lanes // (2 * size) * size + lanes % size
    whole = jnp.where(lanes // (2 * size) <= rows // size, lower, turned)
    work = jnp.where(in_gram, whole, jnp.where(number == rows, 1.0, 0.0))
    pivots, done = [], []
    for base in range(0, count, PANEL):
        height = count - base
        below = lax.broadcasted_iota(jnp.int32, (height, 2 * count), 0)
        columns = [
            jnp.broadcast_to(work[:, at:at + 1], (height, 2 * count))
            for at in ((base + k) // size * 2 * size + (base + k) % size for k in range(PANEL))
        ]
        for k in range(PANEL):
            pivot = columns[k][k:k + 1]
            pivots.append(pivot)
            inverse = 1.0 / pivot
            column = jnp.where(below > k, columns[k], 0.0)
            for m in range(k + 1, PANEL):
                columns[m] = columns[m] - column * (columns[m][k:k + 1] * inverse)
            work = work - column * (work[k:k + 1] * inverse)
        done.append(work[:PANEL])
        work = work[PANEL:]
    work = jnp.concatenate(done, axis=0) * lax.rsqrt(jnp.concatenate(pivots, axis=0))
    inverse = jnp.where(in_gram, pltpu.roll(work, 2 * count - size, 1), work)
    high = inverse.astype(jnp.bfloat16)
    mix[:, :2 * count] = high
    mix[:, 2 * count:] = (inverse - high.astype(jnp.float32)).astype(jnp.bfloat16)
    weights = mix[...]

    def q_write(x):
        return pltpu.make_async_copy(stage.at[x].reshape(count, wy, wz), q_ref.at[:, x], q_sem.at[x])

    def plane(x, carry):
        y_read(x).wait()
        for y in range(0, wy, 2):
            both = jnp.concatenate([y_ref[x, y], y_ref[x, y + 1]], axis=1)
            both = jnp.concatenate([both, both], axis=0)
            out = jnp.dot(weights, both, preferred_element_type=jnp.float32)
            stage[x, pl.ds(y, count, stride=wy), :] = out[:, :wz]
            stage[x, pl.ds(y + 1, count, stride=wy), :] = out[:, wz:]
        q_write(x).start()
        return carry

    lax.fori_loop(0, wx, plane, 0)
    at, to = (lax.broadcasted_iota(jnp.int32, (2 * count, count), d) for d in (0, 1))
    place = (at % (2 * size) < size) & (at // (2 * size) * size + at % size == to)
    r_ref[...] = jnp.dot(
        jnp.where(in_gram & (number >= rows), work, 0.0), jnp.where(place, 1.0, 0.0),
        precision=lax.Precision.HIGHEST, preferred_element_type=jnp.float32,
    )
    for x in range(wx):
        q_write(x).wait()


def body(dims, probes, permeability, absorption, sensitivity, observe_weight):
    count, wx, wy, wz = probes.shape
    size = count // GROUPS
    peers_x, peers_y, chips_x, chips_z = dims
    f32 = jnp.float32
    vmem = pl.BlockSpec(memory_space=pltpu.VMEM)
    hops = peers_y - 1 + chips_x - 1 + chips_z - 1
    half = count // 2
    padded = pltpu.VMEM((GROUPS, wx + 2, wy + 2, size, wz), f32)
    responses, gram = pl.pallas_call(
        functools.partial(respond_kernel, dims),
        out_shape=(
            jax.ShapeDtypeStruct((wx, wy, 2 * count, wz), jnp.bfloat16),
            jax.ShapeDtypeStruct((half, 2 * count), f32),
        ),
        in_specs=[pl.BlockSpec(memory_space=pl.ANY)] * 5,
        out_specs=(pl.BlockSpec(memory_space=pl.ANY), vmem),
        scratch_shapes=[
            pltpu.VMEM((count, wx, wy, wz), jnp.bfloat16),
            pltpu.VMEM((wx, wy, wz), f32),
            pltpu.VMEM((wx, wy, wz), f32),
            pltpu.VMEM((wx, wy, wz), f32),
            pltpu.VMEM((wx, wy, wz), f32),
            padded,
            padded,
            padded,
            pltpu.VMEM((GROUPS, wx, wy, size, wz), f32),
            pltpu.VMEM((wx, wy, 2 * count, wz), jnp.bfloat16),
            pltpu.VMEM((wy * size, wz), f32),
            pltpu.VMEM((wx + 2, wy + 16, wz), f32),
            pltpu.VMEM((2, wx, wz), f32),
            pltpu.VMEM((2, wy, wz), f32),
            pltpu.VMEM((2, wx, wz), f32),
            pltpu.VMEM((2, wx, wz), f32),
            pltpu.VMEM((2, wy, wz), f32),
            pltpu.VMEM((2, wx, wz), f32),
            pltpu.VMEM((9, wx, wy, wz), f32),
            pltpu.VMEM((8, wx, wy, 8, wz), f32),
            pltpu.VMEM((wx + 2, wy + 2, 8, wz), f32),
            pltpu.VMEM((2 * count, 2 * count), f32),
            pltpu.VMEM((peers_y, half, 2 * count), f32),
            pltpu.VMEM((chips_x, half, 2 * count), f32),
            pltpu.VMEM((chips_z, half, 2 * count), f32),
            pltpu.SemaphoreType.DMA((4 + GROUPS,)),
            pltpu.SemaphoreType.DMA((GROUPS,)),
            pltpu.SemaphoreType.DMA((4,)),
            pltpu.SemaphoreType.DMA((4,)),
            pltpu.SemaphoreType.DMA((4,)),
            pltpu.SemaphoreType.DMA((4,)),
            pltpu.SemaphoreType.DMA((2, GROUPS, 4)),
            pltpu.SemaphoreType.DMA((2, GROUPS, 4)),
            pltpu.SemaphoreType.DMA((hops,)),
            pltpu.SemaphoreType.DMA((hops,)),
        ],
        compiler_params=pltpu.CompilerParams(
            collective_id=0, has_side_effects=True, vmem_limit_bytes=60 * 2**20
        ),
    )(probes, permeability, absorption, sensitivity, observe_weight)

    q_basis, r_factor = pl.pallas_call(
        basis_kernel,
        out_shape=(
            jax.ShapeDtypeStruct((count, wx, wy, wz), f32),
            jax.ShapeDtypeStruct((count, count), f32),
        ),
        in_specs=[
            pl.BlockSpec(memory_space=pl.ANY),
            vmem,
        ],
        out_specs=(
            pl.BlockSpec(memory_space=pl.ANY),
            vmem,
        ),
        scratch_shapes=[
            pltpu.VMEM((wx, wy, 2 * count, wz), jnp.bfloat16),
            pltpu.VMEM((count, 4 * count), jnp.bfloat16),
            pltpu.VMEM((wx, count * wy, wz), f32),
            pltpu.SemaphoreType.DMA((wx,)),
            pltpu.SemaphoreType.DMA((wx,)),
        ],
        compiler_params=pltpu.CompilerParams(vmem_limit_bytes=60 * 2**20),
    )(responses, gram)
    return q_basis, r_factor


def solution(mesh):
    peers_x, peers_y = mesh.shape["gx"], mesh.shape["gy"]
    chips_x = 4
    dims = (peers_x, peers_y, chips_x, peers_x // chips_x)
    cell = P("gx", "gy", None)
    field = P(None, "gx", "gy", None)
    return jax.shard_map(
        functools.partial(body, dims),
        mesh=mesh,
        in_specs=(field, cell, cell, cell, cell),
        out_specs=(field, P()),
        check_vma=False,
    )
```

```python
import functools

import jax
import jax.numpy as jnp
from jax import lax
from jax.experimental import pallas as pl
from jax.experimental.pallas import tpu as pltpu
from jax.sharding import PartitionSpec as P

MESH = pl.DeviceIdType.MESH
GROUPS = 4
PANEL = 8


def remote(src, dst, send, recv, where):
    return pltpu.make_async_remote_copy(
        src_ref=src, dst_ref=dst, send_sem=send, recv_sem=recv, device_id=where, device_id_type=MESH
    )


def respond_kernel(
    dims,
    probes_hbm, perm_hbm, absorption_hbm, sensitivity_hbm, weight_hbm,
    y_hbm, gram_out,
    probes, perm, absorption, sensitivity, weight,
    raw, even, odd, rhs, y_out, stage, kpad, kface, khalo_x, khalo_y, sface, shalo_x, shalo_y,
    natural, spread, seed_row, product,
    slot_y, slot_x, slot_z,
    in_sem, out_sem, k_send, k_recv, s_send, s_recv, f_send, f_recv, r_send, r_recv,
):
    peers_x, peers_y, chips_x, chips_z = dims
    count, wx, wy, wz = probes.shape
    size = count // GROUPS
    tiles = size // 8
    gx, gy = lax.axis_index("gx"), lax.axis_index("gy")
    cx, cz = gx // chips_z, gx % chips_z

    x_before = ((gx + peers_x - 1) % peers_x, gy)
    x_after = ((gx + 1) % peers_x, gy)
    y_before = (gx, (gy + peers_y - 1) % peers_y)
    y_after = (gx, (gy + 1) % peers_y)
    def far_first(n):
        return sorted(range(1, n), key=lambda j: -min(j, n - j))

    other_y = [(gx, (gy + j) % peers_y) for j in far_first(peers_y)]
    other_x = [((cx + j) % chips_x * chips_z + cz, gy) for j in far_first(chips_x)]
    other_z = [(cx * chips_z + (cz + j) % chips_z, gy) for j in far_first(chips_z)]

    barrier = pltpu.get_barrier_semaphore()
    everyone = [x_before, x_after, y_before, y_after] + other_y + other_x + other_z
    for where in everyone:
        pl.semaphore_signal(barrier, inc=1, device_id=where, device_id_type=MESH)

    loads = [
        pltpu.make_async_copy(src, dst, in_sem.at[i])
        for i, (src, dst) in enumerate((
            (perm_hbm, perm), (absorption_hbm, absorption), (sensitivity_hbm, sensitivity), (weight_hbm, weight)
        ))
    ]

    def probe_load(g):
        at = pl.ds(g * size, size)
        return pltpu.make_async_copy(probes_hbm.at[at], probes.at[at], in_sem.at[4 + g])

    probe_load(0).start()
    loads[0].start()
    for g in range(1, GROUPS):
        probe_load(g).start()
    for load in loads[1:]:
        load.start()

    fields = (even, odd)

    def faces(e, g):
        mine = (fields[e % 2] if e else raw).at[g]
        sides = (
            (mine.at[wx, pl.ds(1, wy)], mine.at[0, pl.ds(1, wy)], x_after),
            (mine.at[1, pl.ds(1, wy)], mine.at[wx + 1, pl.ds(1, wy)], x_before),
            (mine.at[pl.ds(1, wx), wy], mine.at[pl.ds(1, wx), 0], y_after),
            (mine.at[pl.ds(1, wx), 1], mine.at[pl.ds(1, wx), wy + 1], y_before),
        )
        return [
            remote(src, dst, f_send.at[e % 2, g, i], f_recv.at[e % 2, g, i], where)
            for i, (src, dst, where) in enumerate(sides)
        ]

    def side_rows(pair, halo_x, halo_y, array, send, recv):
        return [
            remote(array.at[wx - 1], halo_x.at[0], send.at[0], recv.at[0], x_after),
            remote(array.at[0], halo_x.at[1], send.at[1], recv.at[1], x_before),
            remote(pair.at[1], halo_y.at[0], send.at[2], recv.at[2], y_after),
            remote(pair.at[0], halo_y.at[1], send.at[3], recv.at[3], y_before),
        ]

    def plane_of(g):
        def plane(x):
            def one(p, carry):
                stage[pl.ds(p, wy, stride=size), :] = probes[g * size + p, x].astype(jnp.float32)
                return carry

            lax.fori_loop(0, size, one, 0, unroll=True)
            raw[g, x + 1, pl.ds(1, wy)] = stage[...].reshape(wy, size, wz)

        return plane

    def outer_planes(g):
        plane = plane_of(g)

        def body(i, carry):
            plane(i * (wx - 1))
            return carry

        probe_load(g).wait()
        lax.fori_loop(0, 2, body, 0)

    def inner_planes(g):
        plane = plane_of(g)

        def body(x, carry):
            plane(x)
            return carry

        lax.fori_loop(1, wx - 1, body, 0)

    def send_x(g):
        for copy in faces(0, g)[:2]:
            copy.start()

    def send_y(g):
        for copy in faces(0, g)[2:]:
            copy.start()

    loads[0].wait()
    kface[0] = perm[:, 0, :]
    kface[1] = perm[:, wy - 1, :]
    k_copies = side_rows(kface, khalo_x, khalo_y, perm, k_send, k_recv)

    outer_planes(0)
    pl.semaphore_wait(barrier, len(everyone))
    for copy in k_copies:
        copy.start()
    send_x(0)
    outer_planes(1)
    send_x(1)
    inner_planes(0)
    send_y(0)
    inner_planes(1)
    send_y(1)

    for load in loads[1:]:
        load.wait()
    for copy in k_copies:
        copy.wait()

    has_x_low = jnp.where(gx > 0, 1.0, 0.0).astype(jnp.float32)
    has_x_high = jnp.where(gx < peers_x - 1, 1.0, 0.0).astype(jnp.float32)
    has_y_low = jnp.where(gy > 0, 1.0, 0.0).astype(jnp.float32)
    has_y_high = jnp.where(gy < peers_y - 1, 1.0, 0.0).astype(jnp.float32)

    center = perm[...]
    kpad[pl.ds(1, wx), pl.ds(8, wy), :] = center
    kpad[0, pl.ds(8, wy), :] = khalo_x[0] * has_x_low
    kpad[wx + 1, pl.ds(8, wy), :] = khalo_x[1] * has_x_high
    for x in range(wx):
        kpad[x + 1, 7:8, :] = khalo_y[0, x:x + 1, :] * has_y_low
        kpad[x + 1, wy + 8:wy + 9, :] = khalo_y[1, x:x + 1, :] * has_y_high
    lane = lax.broadcasted_iota(jnp.int32, (wx, wy, wz), 2)
    x_at = lax.broadcasted_iota(jnp.int32, (wx, wy, wz), 0)
    y_at = lax.broadcasted_iota(jnp.int32, (wx, wy, wz), 1)

    def turned(value, shift):
        flat = pltpu.roll(value.reshape(-1, wz), shift, 1)
        return flat.reshape(value.shape)

    x_low = 0.5 * (center + kpad[pl.ds(0, wx), pl.ds(8, wy), :])
    x_high = 0.5 * (center + kpad[pl.ds(2, wx), pl.ds(8, wy), :])
    y_low = 0.5 * (center + kpad[pl.ds(1, wx), pl.ds(7, wy), :])
    y_high = 0.5 * (center + kpad[pl.ds(1, wx), pl.ds(9, wy), :])
    z_low = 0.5 * (center + jnp.where(lane == 0, 0.0, turned(center, 1)))
    z_high = 0.5 * (center + jnp.where(lane == wz - 1, 0.0, turned(center, wz - 1)))
    diag = absorption[...] + x_low + x_high + y_low + y_high + z_low + z_high
    damp = 0.8 / diag
    seed = damp * sensitivity[...]
    natural[8] = seed
    sface[0] = seed[:, 0, :]
    sface[1] = seed[:, wy - 1, :]
    s_copies = side_rows(sface, shalo_x, shalo_y, natural.at[8], s_send, s_recv)
    for copy in s_copies:
        copy.start()
    for g in range(2, GROUPS):
        outer_planes(g)
        send_x(g)
    for g in range(2, GROUPS):
        inner_planes(g)
        send_y(g)
    natural[0] = damp * jnp.where(x_at == 0, x_low * has_x_low, x_low)
    natural[1] = damp * jnp.where(x_at == wx - 1, x_high * has_x_high, x_high)
    natural[2] = damp * jnp.where(y_at == 0, y_low * has_y_low, y_low)
    natural[3] = damp * jnp.where(y_at == wy - 1, y_high * has_y_high, y_high)
    natural[4] = damp * jnp.where(lane == 0, 0.0, z_low)
    natural[5] = damp * jnp.where(lane == wz - 1, 0.0, z_high)
    natural[6] = damp * weight[...]
    natural[7] = sensitivity[...]

    def widen(x, carry):
        for j in range(9):
            block = natural[j, x]
            for y in range(wy):
                row = jnp.broadcast_to(block[y:y + 1, :], (8, wz))
                if j < 8:
                    spread[j, x, y] = row
                else:
                    seed_row[x + 1, y + 1] = row
        return carry

    lax.fori_loop(0, wx, widen, 0)
    for copy in s_copies:
        copy.wait()
    for side in range(2):
        for y in range(wy):
            seed_row[side * (wx + 1), y + 1] = jnp.broadcast_to(shalo_x[side, y:y + 1, :], (8, wz))
        for x in range(wx):
            seed_row[x + 1, side * (wy + 1)] = jnp.broadcast_to(shalo_y[side, x:x + 1, :], (8, wz))

    def seeded(g, at_x, at_y, n):
        value = raw[g, at_x, at_y].reshape(n, tiles, 8, wz) * seed_row[at_x, at_y].reshape(n, 1, 8, wz)
        return value.reshape(n, size, wz)

    def inside(g, carry):
        def plane(x, carry):
            value = seeded(g, x + 1, pl.ds(1, wy), wy)
            even[g, x + 1, pl.ds(1, wy)] = value
            rhs[g, x] = value
            return carry

        lax.fori_loop(0, wx, plane, 0)
        return carry

    lax.fori_loop(0, GROUPS, inside, 0)

    def inner(act, start):
        return lax.fori_loop(1, wx - 1, act, start)

    def outer(act, start):
        return lax.fori_loop(0, 2, lambda i, carry: act(i * (wx - 1), carry), start)

    def every(act, start):
        return lax.fori_loop(0, wx, act, start)

    def sweep(e, g, last, over):
        old, new = fields[e % 2], fields[(e + 1) % 2]
        shape = (wy, tiles, 8, wz)

        def plane(x):
            def near(dx, dy):
                return old[g, x + 1 + dx, pl.ds(1 + dy, wy)].reshape(shape)

            def factor(j):
                return spread[j, x].reshape(wy, 1, 8, wz)

            here = near(0, 0)
            total = rhs[g, x].reshape(shape) + 0.2 * here
            total = total + factor(0) * near(-1, 0) + factor(1) * near(1, 0)
            total = total + factor(2) * near(0, -1) + factor(3) * near(0, 1)
            total = total + factor(4) * turned(here, 1) + factor(5) * turned(here, wz - 1)
            if last == 2:
                total = (total * factor(7)).reshape(wy, size, wz)
                high = total.astype(jnp.bfloat16).astype(jnp.float32)
                parts = jnp.concatenate([high, total - high], axis=1).astype(jnp.bfloat16)
                y_out[x, :, pl.ds(2 * g * size, 2 * size), :] = parts
                return
            if last == 1:
                total = total * factor(6)
                rhs[g, x] = total.reshape(wy, size, wz)
            new[g, x + 1, pl.ds(1, wy)] = total.reshape(wy, size, wz)

        def planes(x, carry):
            plane(x)
            return carry

        over(planes, 0)

    def step(e, g):
        if e:
            for copy in faces(e - 1, g):
                copy.wait_send()
        for copy in faces(e, g):
            copy.wait_recv()
        if e == 0:
            for side in range(2):
                x, y = side * (wx + 1), side * (wy + 1)
                even[g, x, pl.ds(1, wy)] = seeded(g, x, pl.ds(1, wy), wy)
                even[g, pl.ds(1, wx), y] = seeded(g, pl.ds(1, wx), y, wx)
        sweep(e, g, 1 if e == 2 else 0, every)
        for copy in faces(e + 1, g):
            copy.start()

    def run(e):
        def body(g, carry):
            step(e, g)
            return carry
        lax.fori_loop(0, GROUPS, body, 0)

    for e in range(5):
        run(e)

    def y_write(g):
        at = pl.ds(2 * size * g, 2 * size)
        return pltpu.make_async_copy(y_out.at[:, :, at], y_hbm.at[:, :, at], out_sem.at[g])

    def gram_rows(g, over):
        high_row = 2 * size * (g + 1)

        def add(x, acc):
            for y in range(0, wy, 2):
                both = jnp.concatenate([y_out[x, y, :high_row], y_out[x, y + 1, :high_row]], axis=1)
                acc = acc + lax.dot_general(
                    both[2 * size * g:], both, (((1,), (1,)), ((), ())), preferred_element_type=jnp.float32
                )
            return acc

        return over(add, jnp.zeros((2 * size, high_row), jnp.float32))

    for g in range(GROUPS):
        for copy in faces(4, g):
            copy.wait_send()
        for copy in faces(5, g)[2:]:
            copy.wait_recv()
        sweep(5, g, 2, inner)
        high_row = 2 * size * (g + 1)
        product[2 * size * g:high_row, :high_row] = gram_rows(g, inner)
        if g + 1 < GROUPS:
            product[2 * size * g:high_row, high_row:] = jnp.zeros((2 * size, 2 * count - high_row), jnp.float32)
    for g in range(GROUPS):
        for copy in faces(5, g)[:2]:
            copy.wait_recv()
        sweep(5, g, 2, outer)
        y_write(g).start()
        high_row = 2 * size * (g + 1)
        product[2 * size * g:high_row, :high_row] += gram_rows(g, outer)
    for g in range(GROUPS):
        for copy in faces(5, g):
            copy.wait_send()

    folded = product[...].reshape(GROUPS, 2, size, 2 * count)
    folded = (folded[:, 0] + folded[:, 1]).reshape(count, 2 * count)
    folded = folded + pltpu.roll(folded, 2 * count - size, 1)
    half = count // 2
    first_half = lax.broadcasted_iota(jnp.int32, (half, 2 * count), 1) % (2 * size) < size
    packed = jnp.where(first_half, folded[:half], pltpu.roll(folded[half:], size, 1))
    base, sent = 0, []
    for slots, me, others in (
        (slot_y, gy, other_y), (slot_x, cx, other_x), (slot_z, cz, other_z)
    ):
        n = len(others) + 1
        slots[me] = packed
        copies = [
            remote(slots.at[me], slots.at[me], r_send.at[base + j], r_recv.at[base + j], where)
            for j, where in enumerate(others)
        ]
        for copy in copies:
            copy.start()
        sent += copies
        for copy in copies:
            copy.wait_recv()
        packed = slots[0]
        for j in range(1, n):
            packed = packed + slots[j]
        base += n - 1
    cells = float(wx * peers_x * wy * peers_y * wz)
    gram_out[...] = packed / cells
    for copy in sent:
        copy.wait_send()
    for g in range(GROUPS):
        y_write(g).wait()


def basis_kernel(y_hbm, gram_ref, q_ref, r_ref, y_ref, mix, stage, y_sem, q_sem):
    count = q_ref.shape[0]
    wx = q_ref.shape[1]
    half = count // 2
    size = count // GROUPS
    wy, wz = q_ref.shape[2], q_ref.shape[3]

    def y_read(n):
        return pltpu.make_async_copy(y_hbm.at[n], y_ref.at[n], y_sem.at[n])

    for n in range(wx):
        y_read(n).start()
    packed = gram_ref[...]
    wide = (count, 2 * count)
    rows, lanes = (lax.broadcasted_iota(jnp.int32, wide, d) for d in (0, 1))
    lower = jnp.concatenate([packed, pltpu.roll(packed, 2 * count - size, 1)], axis=0)
    pairs = lower.reshape(GROUPS, 1, size, 2 * count)
    turned = jnp.transpose(jnp.concatenate([pairs, pairs], axis=1).reshape(2 * count, 2 * count))
    turned = turned.reshape(GROUPS, 2, size, 2 * count)[:, 0].reshape(count, 2 * count)
    in_gram = lanes % (2 * size) < size
    number = lanes // (2 * size) * size + lanes % size
    whole = jnp.where(lanes // (2 * size) <= rows // size, lower, turned)
    work = jnp.where(in_gram, whole, jnp.where(number == rows, 1.0, 0.0))
    pivots, done = [], []
    for base in range(0, count, PANEL):
        height = count - base
        below = lax.broadcasted_iota(jnp.int32, (height, 2 * count), 0)
        columns = [
            jnp.broadcast_to(work[:, at:at + 1], (height, 2 * count))
            for at in ((base + k) // size * 2 * size + (base + k) % size for k in range(PANEL))
        ]
        for k in range(PANEL):
            pivot = columns[k][k:k + 1]
            pivots.append(pivot)
            inverse = 1.0 / pivot
            column = jnp.where(below > k, columns[k], 0.0)
            for m in range(k + 1, PANEL):
                columns[m] = columns[m] - column * (columns[m][k:k + 1] * inverse)
            work = work - column * (work[k:k + 1] * inverse)
        done.append(work[:PANEL])
        work = work[PANEL:]
    work = jnp.concatenate(done, axis=0) * lax.rsqrt(jnp.concatenate(pivots, axis=0))
    inverse = jnp.where(in_gram, pltpu.roll(work, 2 * count - size, 1), work)
    high = inverse.astype(jnp.bfloat16)
    mix[:, :2 * count] = high
    mix[:, 2 * count:] = (inverse - high.astype(jnp.float32)).astype(jnp.bfloat16)
    weights = mix[...]

    def q_write(x):
        return pltpu.make_async_copy(stage.at[x].reshape(count, wy, wz), q_ref.at[:, x], q_sem.at[x])

    def plane(x, carry):
        y_read(x).wait()
        for y in range(0, wy, 2):
            both = jnp.concatenate([y_ref[x, y], y_ref[x, y + 1]], axis=1)
            both = jnp.concatenate([both, both], axis=0)
            out = jnp.dot(weights, both, preferred_element_type=jnp.float32)
            stage[x, pl.ds(y, count, stride=wy), :] = out[:, :wz]
            stage[x, pl.ds(y + 1, count, stride=wy), :] = out[:, wz:]
        q_write(x).start()
        return carry

    lax.fori_loop(0, wx, plane, 0)
    at, to = (lax.broadcasted_iota(jnp.int32, (2 * count, count), d) for d in (0, 1))
    place = (at % (2 * size) < size) & (at // (2 * size) * size + at % size == to)
    r_ref[...] = jnp.dot(
        jnp.where(in_gram & (number >= rows), work, 0.0), jnp.where(place, 1.0, 0.0),
        precision=lax.Precision.HIGHEST, preferred_element_type=jnp.float32,
    )
    for x in range(wx):
        q_write(x).wait()


def body(dims, probes, permeability, absorption, sensitivity, observe_weight):
    count, wx, wy, wz = probes.shape
    size = count // GROUPS
    peers_x, peers_y, chips_x, chips_z = dims
    f32 = jnp.float32
    vmem = pl.BlockSpec(memory_space=pltpu.VMEM)
    hops = peers_y - 1 + chips_x - 1 + chips_z - 1
    half = count // 2
    padded = pltpu.VMEM((GROUPS, wx + 2, wy + 2, size, wz), f32)
    responses, gram = pl.pallas_call(
        functools.partial(respond_kernel, dims),
        out_shape=(
            jax.ShapeDtypeStruct((wx, wy, 2 * count, wz), jnp.bfloat16),
            jax.ShapeDtypeStruct((half, 2 * count), f32),
        ),
        in_specs=[pl.BlockSpec(memory_space=pl.ANY)] * 5,
        out_specs=(pl.BlockSpec(memory_space=pl.ANY), vmem),
        scratch_shapes=[
            pltpu.VMEM((count, wx, wy, wz), jnp.bfloat16),
            pltpu.VMEM((wx, wy, wz), f32),
            pltpu.VMEM((wx, wy, wz), f32),
            pltpu.VMEM((wx, wy, wz), f32),
            pltpu.VMEM((wx, wy, wz), f32),
            padded,
            padded,
            padded,
            pltpu.VMEM((GROUPS, wx, wy, size, wz), f32),
            pltpu.VMEM((wx, wy, 2 * count, wz), jnp.bfloat16),
            pltpu.VMEM((wy * size, wz), f32),
            pltpu.VMEM((wx + 2, wy + 16, wz), f32),
            pltpu.VMEM((2, wx, wz), f32),
            pltpu.VMEM((2, wy, wz), f32),
            pltpu.VMEM((2, wx, wz), f32),
            pltpu.VMEM((2, wx, wz), f32),
            pltpu.VMEM((2, wy, wz), f32),
            pltpu.VMEM((2, wx, wz), f32),
            pltpu.VMEM((9, wx, wy, wz), f32),
            pltpu.VMEM((8, wx, wy, 8, wz), f32),
            pltpu.VMEM((wx + 2, wy + 2, 8, wz), f32),
            pltpu.VMEM((2 * count, 2 * count), f32),
            pltpu.VMEM((peers_y, half, 2 * count), f32),
            pltpu.VMEM((chips_x, half, 2 * count), f32),
            pltpu.VMEM((chips_z, half, 2 * count), f32),
            pltpu.SemaphoreType.DMA((4 + GROUPS,)),
            pltpu.SemaphoreType.DMA((GROUPS,)),
            pltpu.SemaphoreType.DMA((4,)),
            pltpu.SemaphoreType.DMA((4,)),
            pltpu.SemaphoreType.DMA((4,)),
            pltpu.SemaphoreType.DMA((4,)),
            pltpu.SemaphoreType.DMA((2, GROUPS, 4)),
            pltpu.SemaphoreType.DMA((2, GROUPS, 4)),
            pltpu.SemaphoreType.DMA((hops,)),
            pltpu.SemaphoreType.DMA((hops,)),
        ],
        compiler_params=pltpu.CompilerParams(
            collective_id=0, has_side_effects=True, vmem_limit_bytes=60 * 2**20
        ),
    )(probes, permeability, absorption, sensitivity, observe_weight)

    q_basis, r_factor = pl.pallas_call(
        basis_kernel,
        out_shape=(
            jax.ShapeDtypeStruct((count, wx, wy, wz), f32),
            jax.ShapeDtypeStruct((count, count), f32),
        ),
        in_specs=[
            pl.BlockSpec(memory_space=pl.ANY),
            vmem,
        ],
        out_specs=(
            pl.BlockSpec(memory_space=pl.ANY),
            vmem,
        ),
        scratch_shapes=[
            pltpu.VMEM((wx, wy, 2 * count, wz), jnp.bfloat16),
            pltpu.VMEM((count, 4 * count), jnp.bfloat16),
            pltpu.VMEM((wx, count * wy, wz), f32),
            pltpu.SemaphoreType.DMA((wx,)),
            pltpu.SemaphoreType.DMA((wx,)),
        ],
        compiler_params=pltpu.CompilerParams(vmem_limit_bytes=60 * 2**20),
    )(responses, gram)
    return q_basis, r_factor


def solution(mesh):
    peers_x, peers_y = mesh.shape["gx"], mesh.shape["gy"]
    chips_x = 4
    dims = (peers_x, peers_y, chips_x, peers_x // chips_x)
    cell = P("gx", "gy", None)
    field = P(None, "gx", "gy", None)
    return jax.shard_map(
        functools.partial(body, dims),
        mesh=mesh,
        in_specs=(field, cell, cell, cell, cell),
        out_specs=(field, P()),
        check_vma=False,
    )
```

```python
import functools

import jax
import jax.numpy as jnp
from jax import lax
from jax.experimental import pallas as pl
from jax.experimental.pallas import tpu as pltpu
from jax.sharding import PartitionSpec as P

MESH = pl.DeviceIdType.MESH
GROUPS = 4
PANEL = 8


def remote(src, dst, send, recv, where):
    return pltpu.make_async_remote_copy(
        src_ref=src, dst_ref=dst, send_sem=send, recv_sem=recv, device_id=where, device_id_type=MESH
    )


def respond_kernel(
    dims,
    probes_hbm, perm_hbm, absorption_hbm, sensitivity_hbm, weight_hbm,
    y_hbm, gram_out,
    probes, perm, absorption, sensitivity, weight,
    raw, even, odd, rhs, y_out, stage, kpad, kface, khalo_x, khalo_y, sface, shalo_x, shalo_y,
    natural, spread, seed_row, product,
    slot_y, slot_x, slot_z,
    in_sem, out_sem, k_send, k_recv, s_send, s_recv, f_send, f_recv, r_send, r_recv,
):
    peers_x, peers_y, chips_x, chips_z = dims
    count, wx, wy, wz = probes.shape
    size = count // GROUPS
    tiles = size // 8
    gx, gy = lax.axis_index("gx"), lax.axis_index("gy")
    cx, cz = gx // chips_z, gx % chips_z

    x_before = ((gx + peers_x - 1) % peers_x, gy)
    x_after = ((gx + 1) % peers_x, gy)
    y_before = (gx, (gy + peers_y - 1) % peers_y)
    y_after = (gx, (gy + 1) % peers_y)
    def far_first(n):
        return sorted(range(1, n), key=lambda j: -min(j, n - j))

    other_y = [(gx, (gy + j) % peers_y) for j in far_first(peers_y)]
    other_x = [((cx + j) % chips_x * chips_z + cz, gy) for j in far_first(chips_x)]
    other_z = [(cx * chips_z + (cz + j) % chips_z, gy) for j in far_first(chips_z)]

    barrier = pltpu.get_barrier_semaphore()
    everyone = [x_before, x_after, y_before, y_after] + other_y + other_x + other_z
    for where in everyone:
        pl.semaphore_signal(barrier, inc=1, device_id=where, device_id_type=MESH)

    loads = [
        pltpu.make_async_copy(src, dst, in_sem.at[i])
        for i, (src, dst) in enumerate((
            (perm_hbm, perm), (absorption_hbm, absorption), (sensitivity_hbm, sensitivity), (weight_hbm, weight)
        ))
    ]

    def probe_load(g):
        at = pl.ds(g * size, size)
        return pltpu.make_async_copy(probes_hbm.at[at], probes.at[at], in_sem.at[4 + g])

    probe_load(0).start()
    loads[0].start()
    for g in range(1, GROUPS):
        probe_load(g).start()
    for load in loads[1:]:
        load.start()

    fields = (even, odd)

    def faces(e, g):
        mine = (fields[e % 2] if e else raw).at[g]
        sides = (
            (mine.at[wx, pl.ds(1, wy)], mine.at[0, pl.ds(1, wy)], x_after),
            (mine.at[1, pl.ds(1, wy)], mine.at[wx + 1, pl.ds(1, wy)], x_before),
            (mine.at[pl.ds(1, wx), wy], mine.at[pl.ds(1, wx), 0], y_after),
            (mine.at[pl.ds(1, wx), 1], mine.at[pl.ds(1, wx), wy + 1], y_before),
        )
        return [
            remote(src, dst, f_send.at[e % 2, g, i], f_recv.at[e % 2, g, i], where)
            for i, (src, dst, where) in enumerate(sides)
        ]

    def side_rows(pair, halo_x, halo_y, array, send, recv):
        return [
            remote(array.at[wx - 1], halo_x.at[0], send.at[0], recv.at[0], x_after),
            remote(array.at[0], halo_x.at[1], send.at[1], recv.at[1], x_before),
            remote(pair.at[1], halo_y.at[0], send.at[2], recv.at[2], y_after),
            remote(pair.at[0], halo_y.at[1], send.at[3], recv.at[3], y_before),
        ]

    def plane_of(g):
        def plane(x):
            def one(p, carry):
                stage[pl.ds(p, wy, stride=size), :] = probes[g * size + p, x].astype(jnp.float32)
                return carry

            lax.fori_loop(0, size, one, 0, unroll=True)
            raw[g, x + 1, pl.ds(1, wy)] = stage[...].reshape(wy, size, wz)

        return plane

    def outer_planes(g):
        plane = plane_of(g)

        def body(i, carry):
            plane(i * (wx - 1))
            return carry

        probe_load(g).wait()
        lax.fori_loop(0, 2, body, 0)

    def inner_planes(g):
        plane = plane_of(g)

        def body(x, carry):
            plane(x)
            return carry

        lax.fori_loop(1, wx - 1, body, 0)

    def send_x(g):
        for copy in faces(0, g)[:2]:
            copy.start()

    def send_y(g):
        for copy in faces(0, g)[2:]:
            copy.start()

    loads[0].wait()
    kface[0] = perm[:, 0, :]
    kface[1] = perm[:, wy - 1, :]
    k_copies = side_rows(kface, khalo_x, khalo_y, perm, k_send, k_recv)

    outer_planes(0)
    pl.semaphore_wait(barrier, len(everyone))
    for copy in k_copies:
        copy.start()
    send_x(0)
    outer_planes(1)
    send_x(1)
    inner_planes(0)
    send_y(0)
    inner_planes(1)
    send_y(1)

    for load in loads[1:]:
        load.wait()
    for copy in k_copies:
        copy.wait()

    has_x_low = jnp.where(gx > 0, 1.0, 0.0).astype(jnp.float32)
    has_x_high = jnp.where(gx < peers_x - 1, 1.0, 0.0).astype(jnp.float32)
    has_y_low = jnp.where(gy > 0, 1.0, 0.0).astype(jnp.float32)
    has_y_high = jnp.where(gy < peers_y - 1, 1.0, 0.0).astype(jnp.float32)

    center = perm[...]
    kpad[pl.ds(1, wx), pl.ds(8, wy), :] = center
    kpad[0, pl.ds(8, wy), :] = khalo_x[0] * has_x_low
    kpad[wx + 1, pl.ds(8, wy), :] = khalo_x[1] * has_x_high
    for x in range(wx):
        kpad[x + 1, 7:8, :] = khalo_y[0, x:x + 1, :] * has_y_low
        kpad[x + 1, wy + 8:wy + 9, :] = khalo_y[1, x:x + 1, :] * has_y_high
    lane = lax.broadcasted_iota(jnp.int32, (wx, wy, wz), 2)
    x_at = lax.broadcasted_iota(jnp.int32, (wx, wy, wz), 0)
    y_at = lax.broadcasted_iota(jnp.int32, (wx, wy, wz), 1)

    def turned(value, shift):
        flat = pltpu.roll(value.reshape(-1, wz), shift, 1)
        return flat.reshape(value.shape)

    x_low = 0.5 * (center + kpad[pl.ds(0, wx), pl.ds(8, wy), :])
    x_high = 0.5 * (center + kpad[pl.ds(2, wx), pl.ds(8, wy), :])
    y_low = 0.5 * (center + kpad[pl.ds(1, wx), pl.ds(7, wy), :])
    y_high = 0.5 * (center + kpad[pl.ds(1, wx), pl.ds(9, wy), :])
    z_low = 0.5 * (center + jnp.where(lane == 0, 0.0, turned(center, 1)))
    z_high = 0.5 * (center + jnp.where(lane == wz - 1, 0.0, turned(center, wz - 1)))
    diag = absorption[...] + x_low + x_high + y_low + y_high + z_low + z_high
    damp = 0.8 / diag
    seed = damp * sensitivity[...]
    natural[8] = seed
    sface[0] = seed[:, 0, :]
    sface[1] = seed[:, wy - 1, :]
    s_copies = side_rows(sface, shalo_x, shalo_y, natural.at[8], s_send, s_recv)
    for copy in s_copies:
        copy.start()
    for g in range(2, GROUPS):
        outer_planes(g)
        send_x(g)
    for g in range(2, GROUPS):
        inner_planes(g)
        send_y(g)
    natural[0] = damp * jnp.where(x_at == 0, x_low * has_x_low, x_low)
    natural[1] = damp * jnp.where(x_at == wx - 1, x_high * has_x_high, x_high)
    natural[2] = damp * jnp.where(y_at == 0, y_low * has_y_low, y_low)
    natural[3] = damp * jnp.where(y_at == wy - 1, y_high * has_y_high, y_high)
    natural[4] = damp * jnp.where(lane == 0, 0.0, z_low)
    natural[5] = damp * jnp.where(lane == wz - 1, 0.0, z_high)
    natural[6] = damp * weight[...]
    natural[7] = sensitivity[...]

    def widen(x, carry):
        for j in range(9):
            block = natural[j, x]
            for y in range(wy):
                row = jnp.broadcast_to(block[y:y + 1, :], (8, wz))
                if j < 8:
                    spread[j, x, y] = row
                else:
                    seed_row[x + 1, y + 1] = row
        return carry

    lax.fori_loop(0, wx, widen, 0)
    for copy in s_copies:
        copy.wait()
    for side in range(2):
        for y in range(wy):
            seed_row[side * (wx + 1), y + 1] = jnp.broadcast_to(shalo_x[side, y:y + 1, :], (8, wz))
        for x in range(wx):
            seed_row[x + 1, side * (wy + 1)] = jnp.broadcast_to(shalo_y[side, x:x + 1, :], (8, wz))

    def seeded(g, at_x, at_y, n):
        value = raw[g, at_x, at_y].reshape(n, tiles, 8, wz) * seed_row[at_x, at_y].reshape(n, 1, 8, wz)
        return value.reshape(n, size, wz)

    def inside(g, carry):
        def plane(x, carry):
            value = seeded(g, x + 1, pl.ds(1, wy), wy)
            even[g, x + 1, pl.ds(1, wy)] = value
            rhs[g, x] = value
            return carry

        lax.fori_loop(0, wx, plane, 0)
        return carry

    lax.fori_loop(0, GROUPS, inside, 0)

    def inner(act, start):
        return lax.fori_loop(1, wx - 1, act, start)

    def outer(act, start):
        return lax.fori_loop(0, 2, lambda i, carry: act(i * (wx - 1), carry), start, unroll=True)

    def every(act, start):
        return lax.fori_loop(0, wx, act, start)

    def sweep(e, g, last, over):
        old, new = fields[e % 2], fields[(e + 1) % 2]
        shape = (wy, tiles, 8, wz)

        def plane(x):
            def near(dx, dy):
                return old[g, x + 1 + dx, pl.ds(1 + dy, wy)].reshape(shape)

            def factor(j):
                return spread[j, x].reshape(wy, 1, 8, wz)

            here = near(0, 0)
            total = rhs[g, x].reshape(shape) + 0.2 * here
            total = total + factor(0) * near(-1, 0) + factor(1) * near(1, 0)
            total = total + factor(2) * near(0, -1) + factor(3) * near(0, 1)
            total = total + factor(4) * turned(here, 1) + factor(5) * turned(here, wz - 1)
            if last == 2:
                total = (total * factor(7)).reshape(wy, size, wz)
                high = total.astype(jnp.bfloat16).astype(jnp.float32)
                parts = jnp.concatenate([high, total - high], axis=1).astype(jnp.bfloat16)
                y_out[x, :, pl.ds(2 * g * size, 2 * size), :] = parts
                return
            if last == 1:
                total = total * factor(6)
                rhs[g, x] = total.reshape(wy, size, wz)
            new[g, x + 1, pl.ds(1, wy)] = total.reshape(wy, size, wz)

        def planes(x, carry):
            plane(x)
            return carry

        over(planes, 0)

    def step(e, g):
        if e:
            for copy in faces(e - 1, g):
                copy.wait_send()
        for copy in faces(e, g):
            copy.wait_recv()
        if e == 0:
            for side in range(2):
                x, y = side * (wx + 1), side * (wy + 1)
                even[g, x, pl.ds(1, wy)] = seeded(g, x, pl.ds(1, wy), wy)
                even[g, pl.ds(1, wx), y] = seeded(g, pl.ds(1, wx), y, wx)
        sweep(e, g, 1 if e == 2 else 0, every)
        for copy in faces(e + 1, g):
            copy.start()

    def run(e):
        def body(g, carry):
            step(e, g)
            return carry
        lax.fori_loop(0, GROUPS, body, 0)

    for e in range(5):
        run(e)

    def y_write(g):
        at = pl.ds(2 * size * g, 2 * size)
        return pltpu.make_async_copy(y_out.at[:, :, at], y_hbm.at[:, :, at], out_sem.at[g])

    def gram_rows(g, over):
        high_row = 2 * size * (g + 1)

        def add(x, acc):
            for y in range(0, wy, 2):
                both = jnp.concatenate([y_out[x, y, :high_row], y_out[x, y + 1, :high_row]], axis=1)
                acc = acc + lax.dot_general(
                    both[2 * size * g:], both, (((1,), (1,)), ((), ())), preferred_element_type=jnp.float32
                )
            return acc

        return over(add, jnp.zeros((2 * size, high_row), jnp.float32))

    for g in range(GROUPS):
        for copy in faces(4, g):
            copy.wait_send()
        for copy in faces(5, g)[2:]:
            copy.wait_recv()
        sweep(5, g, 2, inner)
        high_row = 2 * size * (g + 1)
        product[2 * size * g:high_row, :high_row] = gram_rows(g, inner)
        if g + 1 < GROUPS:
            product[2 * size * g:high_row, high_row:] = jnp.zeros((2 * size, 2 * count - high_row), jnp.float32)
    for g in range(GROUPS):
        for copy in faces(5, g)[:2]:
            copy.wait_recv()
        sweep(5, g, 2, outer)
        y_write(g).start()
        high_row = 2 * size * (g + 1)
        product[2 * size * g:high_row, :high_row] += gram_rows(g, outer)
    for g in range(GROUPS):
        for copy in faces(5, g):
            copy.wait_send()

    folded = product[...].reshape(GROUPS, 2, size, 2 * count)
    folded = (folded[:, 0] + folded[:, 1]).reshape(count, 2 * count)
    folded = folded + pltpu.roll(folded, 2 * count - size, 1)
    half = count // 2
    first_half = lax.broadcasted_iota(jnp.int32, (half, 2 * count), 1) % (2 * size) < size
    packed = jnp.where(first_half, folded[:half], pltpu.roll(folded[half:], size, 1))
    base, sent = 0, []
    for slots, me, others in (
        (slot_y, gy, other_y), (slot_x, cx, other_x), (slot_z, cz, other_z)
    ):
        n = len(others) + 1
        slots[me] = packed
        copies = [
            remote(slots.at[me], slots.at[me], r_send.at[base + j], r_recv.at[base + j], where)
            for j, where in enumerate(others)
        ]
        for copy in copies:
            copy.start()
        sent += copies
        for copy in copies:
            copy.wait_recv()
        packed = slots[0]
        for j in range(1, n):
            packed = packed + slots[j]
        base += n - 1
    cells = float(wx * peers_x * wy * peers_y * wz)
    gram_out[...] = packed / cells
    for copy in sent:
        copy.wait_send()
    for g in range(GROUPS):
        y_write(g).wait()


def basis_kernel(y_hbm, gram_ref, q_ref, r_ref, y_ref, mix, stage, y_sem, q_sem):
    count = q_ref.shape[0]
    wx = q_ref.shape[1]
    half = count // 2
    size = count // GROUPS
    wy, wz = q_ref.shape[2], q_ref.shape[3]

    def y_read(n):
        return pltpu.make_async_copy(y_hbm.at[n], y_ref.at[n], y_sem.at[n])

    for n in range(wx):
        y_read(n).start()
    packed = gram_ref[...]
    wide = (count, 2 * count)
    rows, lanes = (lax.broadcasted_iota(jnp.int32, wide, d) for d in (0, 1))
    lower = jnp.concatenate([packed, pltpu.roll(packed, 2 * count - size, 1)], axis=0)
    pairs = lower.reshape(GROUPS, 1, size, 2 * count)
    turned = jnp.transpose(jnp.concatenate([pairs, pairs], axis=1).reshape(2 * count, 2 * count))
    turned = turned.reshape(GROUPS, 2, size, 2 * count)[:, 0].reshape(count, 2 * count)
    in_gram = lanes % (2 * size) < size
    number = lanes // (2 * size) * size + lanes % size
    whole = jnp.where(lanes // (2 * size) <= rows // size, lower, turned)
    work = jnp.where(in_gram, whole, jnp.where(number == rows, 1.0, 0.0))
    pivots, done = [], []
    for base in range(0, count, PANEL):
        height = count - base
        below = lax.broadcasted_iota(jnp.int32, (height, 2 * count), 0)
        columns = [
            jnp.broadcast_to(work[:, at:at + 1], (height, 2 * count))
            for at in ((base + k) // size * 2 * size + (base + k) % size for k in range(PANEL))
        ]
        for k in range(PANEL):
            pivot = columns[k][k:k + 1]
            pivots.append(pivot)
            inverse = 1.0 / pivot
            column = jnp.where(below > k, columns[k], 0.0)
            for m in range(k + 1, PANEL):
                columns[m] = columns[m] - column * (columns[m][k:k + 1] * inverse)
            work = work - column * (work[k:k + 1] * inverse)
        done.append(work[:PANEL])
        work = work[PANEL:]
    work = jnp.concatenate(done, axis=0) * lax.rsqrt(jnp.concatenate(pivots, axis=0))
    inverse = jnp.where(in_gram, pltpu.roll(work, 2 * count - size, 1), work)
    high = inverse.astype(jnp.bfloat16)
    mix[:, :2 * count] = high
    mix[:, 2 * count:] = (inverse - high.astype(jnp.float32)).astype(jnp.bfloat16)
    weights = mix[...]

    def q_write(x):
        return pltpu.make_async_copy(stage.at[x].reshape(count, wy, wz), q_ref.at[:, x], q_sem.at[x])

    def plane(x, carry):
        y_read(x).wait()
        for y in range(0, wy, 2):
            both = jnp.concatenate([y_ref[x, y], y_ref[x, y + 1]], axis=1)
            both = jnp.concatenate([both, both], axis=0)
            out = jnp.dot(weights, both, preferred_element_type=jnp.float32)
            stage[x, pl.ds(y, count, stride=wy), :] = out[:, :wz]
            stage[x, pl.ds(y + 1, count, stride=wy), :] = out[:, wz:]
        q_write(x).start()
        return carry

    lax.fori_loop(0, wx, plane, 0)
    at, to = (lax.broadcasted_iota(jnp.int32, (2 * count, count), d) for d in (0, 1))
    place = (at % (2 * size) < size) & (at // (2 * size) * size + at % size == to)
    r_ref[...] = jnp.dot(
        jnp.where(in_gram & (number >= rows), work, 0.0), jnp.where(place, 1.0, 0.0),
        precision=lax.Precision.HIGHEST, preferred_element_type=jnp.float32,
    )
    for x in range(wx):
        q_write(x).wait()


def body(dims, probes, permeability, absorption, sensitivity, observe_weight):
    count, wx, wy, wz = probes.shape
    size = count // GROUPS
    peers_x, peers_y, chips_x, chips_z = dims
    f32 = jnp.float32
    vmem = pl.BlockSpec(memory_space=pltpu.VMEM)
    hops = peers_y - 1 + chips_x - 1 + chips_z - 1
    half = count // 2
    padded = pltpu.VMEM((GROUPS, wx + 2, wy + 2, size, wz), f32)
    responses, gram = pl.pallas_call(
        functools.partial(respond_kernel, dims),
        out_shape=(
            jax.ShapeDtypeStruct((wx, wy, 2 * count, wz), jnp.bfloat16),
            jax.ShapeDtypeStruct((half, 2 * count), f32),
        ),
        in_specs=[pl.BlockSpec(memory_space=pl.ANY)] * 5,
        out_specs=(pl.BlockSpec(memory_space=pl.ANY), vmem),
        scratch_shapes=[
            pltpu.VMEM((count, wx, wy, wz), jnp.bfloat16),
            pltpu.VMEM((wx, wy, wz), f32),
            pltpu.VMEM((wx, wy, wz), f32),
            pltpu.VMEM((wx, wy, wz), f32),
            pltpu.VMEM((wx, wy, wz), f32),
            padded,
            padded,
            padded,
            pltpu.VMEM((GROUPS, wx, wy, size, wz), f32),
            pltpu.VMEM((wx, wy, 2 * count, wz), jnp.bfloat16),
            pltpu.VMEM((wy * size, wz), f32),
            pltpu.VMEM((wx + 2, wy + 16, wz), f32),
            pltpu.VMEM((2, wx, wz), f32),
            pltpu.VMEM((2, wy, wz), f32),
            pltpu.VMEM((2, wx, wz), f32),
            pltpu.VMEM((2, wx, wz), f32),
            pltpu.VMEM((2, wy, wz), f32),
            pltpu.VMEM((2, wx, wz), f32),
            pltpu.VMEM((9, wx, wy, wz), f32),
            pltpu.VMEM((8, wx, wy, 8, wz), f32),
            pltpu.VMEM((wx + 2, wy + 2, 8, wz), f32),
            pltpu.VMEM((2 * count, 2 * count), f32),
            pltpu.VMEM((peers_y, half, 2 * count), f32),
            pltpu.VMEM((chips_x, half, 2 * count), f32),
            pltpu.VMEM((chips_z, half, 2 * count), f32),
            pltpu.SemaphoreType.DMA((4 + GROUPS,)),
            pltpu.SemaphoreType.DMA((GROUPS,)),
            pltpu.SemaphoreType.DMA((4,)),
            pltpu.SemaphoreType.DMA((4,)),
            pltpu.SemaphoreType.DMA((4,)),
            pltpu.SemaphoreType.DMA((4,)),
            pltpu.SemaphoreType.DMA((2, GROUPS, 4)),
            pltpu.SemaphoreType.DMA((2, GROUPS, 4)),
            pltpu.SemaphoreType.DMA((hops,)),
            pltpu.SemaphoreType.DMA((hops,)),
        ],
        compiler_params=pltpu.CompilerParams(
            collective_id=0, has_side_effects=True, vmem_limit_bytes=60 * 2**20
        ),
    )(probes, permeability, absorption, sensitivity, observe_weight)

    q_basis, r_factor = pl.pallas_call(
        basis_kernel,
        out_shape=(
            jax.ShapeDtypeStruct((count, wx, wy, wz), f32),
            jax.ShapeDtypeStruct((count, count), f32),
        ),
        in_specs=[
            pl.BlockSpec(memory_space=pl.ANY),
            vmem,
        ],
        out_specs=(
            pl.BlockSpec(memory_space=pl.ANY),
            vmem,
        ),
        scratch_shapes=[
            pltpu.VMEM((wx, wy, 2 * count, wz), jnp.bfloat16),
            pltpu.VMEM((count, 4 * count), jnp.bfloat16),
            pltpu.VMEM((wx, count * wy, wz), f32),
            pltpu.SemaphoreType.DMA((wx,)),
            pltpu.SemaphoreType.DMA((wx,)),
        ],
        compiler_params=pltpu.CompilerParams(vmem_limit_bytes=60 * 2**20),
    )(responses, gram)
    return q_basis, r_factor


def solution(mesh):
    peers_x, peers_y = mesh.shape["gx"], mesh.shape["gy"]
    chips_x = 4
    dims = (peers_x, peers_y, chips_x, peers_x // chips_x)
    cell = P("gx", "gy", None)
    field = P(None, "gx", "gy", None)
    return jax.shard_map(
        functools.partial(body, dims),
        mesh=mesh,
        in_specs=(field, cell, cell, cell, cell),
        out_specs=(field, P()),
        check_vma=False,
    )
```
